32 devices in a mesh: dp: 8 (over z, core), expert: 4 (over y, x).
Axes of the slice: x: 2, y: 2, z: 4, core: 2. Of those that a mesh axis runs over, the one named last changes fastest.
Arguments:
- tokens: bfloat16 [4096, 2048], P(('dp', 'expert')), may hold values from -6 to 6
- cotangent: bfloat16 [4096, 2048], P(('dp', 'expert')), may hold values from -6 to 6
- expert_ids: int32 [4096, 2], P(('dp', 'expert')), may hold values from 0 to 3, all different within a row; in each aligned block of 128 rows (0 to 127, 128 to 255, ...) at most 80 rows name the same one
- gate_weights: float32 [4096, 2], P(('dp', 'expert')), may hold values from 0.1 to 1
- partner: int32 [4], replicated, may hold values from 0 to 3, as said below
- w_gate: bfloat16 [4, 2048, 768], P('expert'), may hold values from -0.125 to 0.125
- w_up: bfloat16 [4, 2048, 768], P('expert'), may hold values from -0.125 to 0.125
- w_down: bfloat16 [4, 768, 2048], P('expert'), may hold values from -0.21875 to 0.21875
Outputs:
- mixed_out: bfloat16 [4096, 2048], P(('dp', 'expert'))
- token_grad: bfloat16 [4096, 2048], P(('dp', 'expert'))
- gate_grad: float32 [4096, 2], P(('dp', 'expert'))
- slot_grad_gate: float32 [4, 2048, 768], P('expert', 'dp')
- slot_grad_up: float32 [4, 2048, 768], P('expert', 'dp')
- slot_grad_down: float32 [4, 768, 2048], P('expert', None, 'dp')
The draws below stay inside these ranges and needn't reach their ends.
Inputs may be any that keep to these rules, and one draw needn't show every extreme that they name: `expert_ids`: each row names 2 different experts. Among the 128 rows of one device no expert is named by more than 80 rows, and in every draw some device names some expert exactly 80 times. partner[partner[i]] = i and partner[i] != i for every slot i.
All inputs are finite; a program needn't handle non-finite values.
Results may differ from the reference program's by a relative error of at most 0.015.
Values may be sent and summed in bfloat16 or wider, within the bound.
No kernel may reach another device: no remote copies, remote signals or barrier semaphores. Data moves between devices by JAX's collectives and lax.ppermute only.
A program may use at most 128 MiB of HBM per device.

```python
import math
import jax
import jax.numpy as jnp
import numpy as np
from jax import lax

D = 2048
FF = 768
TOPK = 2
TOK_DEV = 128
EXPERTS = 4
CAP = 80
TOKENS = 4096
N_DP = 8


def draw_partner(key, part):
    order = jax.random.permutation(key, EXPERTS).astype(jnp.int32)
    positions = jnp.arange(EXPERTS, dtype=jnp.int32)
    mates = order[positions ^ 1]
    return jnp.zeros((EXPERTS,), jnp.int32).at[order].set(mates)


def strengthened(values, rng, source, target, shards_of, factor):
    def block_of(dim):
        return (jnp.arange(values.shape[dim]) // (values.shape[dim] // shards_of)).reshape((-1,) + (1,) * (values.ndim - 1 - dim))

    first = jax.random.permutation(rng, shards_of)[block_of(target)]
    second = (block_of(target) + shards_of // 2) % shards_of
    return jnp.where((block_of(source) == first) | (block_of(source) == second), factor * values, values)


def steps_of(own_key, extent, pieces, low, largest):
    loudness, own = 1.0, jax.random.fold_in(own_key, 6)
    for dim, blocks in pieces:
        heights = jnp.exp(jax.random.uniform(jax.random.fold_in(own, dim), (blocks,), jnp.float32, low / len(pieces), largest / len(pieces)))
        loudness = loudness * jnp.repeat(heights, extent[dim] // blocks).reshape([-1 if axis == dim else 1 for axis in range(len(extent))])
    return loudness


def assign_block(stream_key, own, number, rows, number_of, top, reach, lean):
    sequence = jax.random.permutation(stream_key, number_of)
    crowded, common = shares(number_of, rows * top, reach, lean, True), shares(number_of, rows * top, reach, lean, False)
    places = jnp.arange(number_of)

    def named(lengths, turn):
        used = int((lengths > 0).sum())
        fixed = max(1, used // 4)
        shifted = fixed + (places - fixed + turn * (used - fixed)) % max(1, number_of - fixed)
        return jnp.zeros((number_of,), jnp.int32).at[sequence[jnp.where(places < fixed, places, shifted)]].set(jnp.asarray(lengths, jnp.int32))

    lengths = jnp.where(number % 4 == 0, named(crowded, number // 4), named(common, number - number // 4 - 1))
    mixed = jax.random.permutation(jax.random.fold_in(own, 3), number_of)
    source_of, taker = mixed[0:number_of // 2 * 2:2], mixed[1:number_of // 2 * 2:2]
    margin = jnp.minimum(lengths[source_of] - 1, reach - lengths[taker]) // 2
    margin = jnp.where((source_of == sequence[0]) | (taker == sequence[0]) | (lengths[taker] == 0), 0, jnp.maximum(margin, 0))
    shifted = jax.random.randint(jax.random.fold_in(own, 4), (number_of // 2,), 0, 1 << 20) % (margin + 1)
    lengths = lengths.at[source_of].add(-shifted).at[taker].add(shifted)
    labels = jnp.searchsorted(jnp.cumsum(lengths), jnp.arange(rows * top), side="right").astype(jnp.int32)
    grid = labels.reshape(top, rows).T
    grid = grid[jax.random.permutation(jax.random.fold_in(own, 1), rows)]
    turn = jax.random.randint(jax.random.fold_in(own, 2), (rows, 1), 0, top)
    return jnp.take_along_axis(grid, (jnp.arange(top)[None, :] + turn) % top, axis=1)


def shares(count, total, bound, lean, full):
    weights = [(1 << 20) // math.isqrt(standing ** lean) + 1 for standing in range(1, count + 1)]
    largest = bound if full else min(bound, max(-(-total // count), total * weights[0] // sum(weights)))
    least = 1 if total - largest >= count - 1 else 0
    given, rest = [largest] + [least] * (count - 1), total - largest - least * (count - 1)
    while rest > 0:
        candidates = [i for i in range(1, count) if given[i] < largest] or [i for i in range(1, count) if given[i] < bound]
        mass, left = sum([weights[i] for i in candidates]), rest
        for i in candidates:
            extra = min(bound - given[i], max(1, left * weights[i] // mass), rest)
            given[i] = given[i] + extra
            rest = rest - extra
    return np.array(given)


def noise(stream_key, shape, spread, bound, shards=(), kind=jnp.bfloat16):
    entries = jax.random.normal(stream_key, shape, jnp.float32) * spread
    if len(shards) > 0:
        entries = steps_of(stream_key, shape, shards, -0.22, 0.18) * entries
    return jnp.clip(entries, min=-bound, max=bound).astype(kind)


def gaussian_with(key, shape, spread, reach, split, heavy, held_as=jnp.bfloat16):
    entries = spread * jax.random.normal(key, shape, jnp.float32)
    if split:
        entries = entries * steps_of(key, shape, split, -0.22, 0.18)
    return jnp.clip(strengthened(entries, jax.random.fold_in(key, 3), *heavy), -reach, reach).astype(held_as)


def setup_inputs(seed: int = 0) -> dict:
    streams_of = jax.random.split(jax.random.key(seed), 9)
    tokens = gaussian_with(streams_of[0], (TOKENS, D), 1.0, 6.0, ((0, 32),), (0, 1, 32, 2.75))
    cotangent = gaussian_with(streams_of[1], (TOKENS, D), 1.0, 6.0, ((0, 32),), (0, 1, 32, 2.75))
    expert_ids_keys = jax.random.split(jax.random.fold_in(streams_of[2], 1), TOKENS // TOK_DEV)
    expert_ids_turns = jax.random.permutation(jax.random.fold_in(streams_of[2], 3), TOKENS // TOK_DEV)
    expert_ids = jax.vmap(lambda own, number: assign_block(jax.random.fold_in(streams_of[2], 2), own, number, TOK_DEV, EXPERTS, TOPK, CAP, 2))(expert_ids_keys, expert_ids_turns).reshape((TOKENS, TOPK))
    gate_weights = jnp.clip(jnp.exp(math.log(1.0) - 2.3025851 * jax.random.uniform(streams_of[3], (TOKENS, TOPK), jnp.float32) ** steps_of(streams_of[3], (TOKENS, TOPK), ((0, 32),), -0.2, 0.2)), 0.1, 1.0)
    partner = draw_partner(jax.random.fold_in(streams_of[8], 71), 0)
    w_gate = noise(streams_of[5], (EXPERTS, D, FF), D ** -0.5, 0.125, ((0, 4),))
    w_up = noise(streams_of[6], (EXPERTS, D, FF), D ** -0.5, 0.125, ((0, 4),))
    w_down = noise(streams_of[7], (EXPERTS, FF, D), FF ** -0.5, 0.21875, ((0, 4),))
    return dict(tokens=tokens, cotangent=cotangent, expert_ids=expert_ids, gate_weights=gate_weights, partner=partner, w_gate=w_gate, w_up=w_up, w_down=w_down)


def assign_slots(block_ids):
    flat_ids = block_ids.reshape(-1).astype(jnp.int32)
    one_hot = (flat_ids[:, None] == jnp.arange(EXPERTS, dtype=jnp.int32)[None, :]).astype(jnp.int32)
    earlier = (jnp.cumsum(one_hot, axis=0) - one_hot).astype(jnp.int32)
    position = jnp.sum(earlier * one_hot, axis=1).astype(jnp.int32)
    return (flat_ids * CAP + position).astype(jnp.int32)


def expert_pass(row_data, grads_in, gate_mat, up_mat, down_mat):
    gate_pre = jnp.dot(row_data, gate_mat, preferred_element_type=jnp.float32)
    up_pre = jnp.dot(row_data, up_mat, preferred_element_type=jnp.float32)
    sigmoid_gate = jax.nn.sigmoid(gate_pre)
    hidden = (gate_pre * sigmoid_gate * up_pre).astype(jnp.bfloat16)
    expert_out = jnp.dot(hidden, down_mat, preferred_element_type=jnp.float32).astype(jnp.bfloat16)
    hidden_grad = jnp.dot(grads_in, down_mat.T, preferred_element_type=jnp.float32)
    gate_grad_pre = (hidden_grad * up_pre * sigmoid_gate * (1.0 + gate_pre * (1.0 - sigmoid_gate))).astype(jnp.bfloat16)
    up_grad_pre = (hidden_grad * gate_pre * sigmoid_gate).astype(jnp.bfloat16)
    row_grad = (jnp.dot(gate_grad_pre, gate_mat.T, preferred_element_type=jnp.float32)
                + jnp.dot(up_grad_pre, up_mat.T, preferred_element_type=jnp.float32)).astype(jnp.bfloat16)
    part_gate = jnp.dot(row_data.T, gate_grad_pre, preferred_element_type=jnp.float32)
    part_up = jnp.dot(row_data.T, up_grad_pre, preferred_element_type=jnp.float32)
    part_down = jnp.dot(hidden.T, grads_in, preferred_element_type=jnp.float32)
    return expert_out, row_grad, part_gate, part_up, part_down


def take_rows(source_tab, index_tab):
    return jax.vmap(lambda one_tab, one_index: one_tab[one_index])(source_tab, index_tab)


def by_expert(buffered):
    return buffered.reshape(EXPERTS, EXPERTS, CAP, D).transpose(1, 0, 2, 3).reshape(EXPERTS, EXPERTS * CAP, D)


def reference(tokens, cotangent, expert_ids, gate_weights, partner, w_gate, w_up, w_down):
    per_row = EXPERTS * TOK_DEV
    assigns = TOK_DEV * TOPK

    def one_row(totals, row_input):
        row_tokens, row_cot, row_ids, row_gates = row_input
        slot_index = jax.vmap(assign_slots)(row_ids.reshape(EXPERTS, TOK_DEV, TOPK))
        repeated = jnp.repeat(row_tokens.reshape(EXPERTS, TOK_DEV, D), TOPK, axis=1)
        cot_float = row_cot.astype(jnp.float32)
        scaled = (row_gates[:, :, None] * cot_float[:, None, :]).astype(jnp.bfloat16).reshape(EXPERTS, assigns, D)
        filler = jnp.full((EXPERTS, EXPERTS * CAP), assigns, dtype=jnp.int32)
        source_ids = jnp.broadcast_to(jnp.arange(EXPERTS, dtype=jnp.int32)[:, None], (EXPERTS, assigns))
        assign_ids = jnp.broadcast_to(jnp.arange(assigns, dtype=jnp.int32)[None, :], (EXPERTS, assigns))
        lookup = filler.at[source_ids, slot_index].set(assign_ids)
        zero_row = jnp.zeros((EXPERTS, 1, D), jnp.bfloat16)
        buffer_x = take_rows(jnp.concatenate([repeated, zero_row], axis=1), lookup)
        buffer_g = take_rows(jnp.concatenate([scaled, zero_row], axis=1), lookup)
        results = lax.map(lambda item: expert_pass(*item),
                          (by_expert(buffer_x), by_expert(buffer_g), w_gate, w_up, w_down))
        expert_out, row_grad, part_gate, part_up, part_down = results
        per_assign = take_rows(by_expert(expert_out), slot_index).astype(jnp.float32).reshape(per_row, TOPK, D)
        mixed_out = jnp.sum(row_gates[:, :, None] * per_assign, axis=1).astype(jnp.bfloat16)
        gate_grad = jnp.sum(cot_float[:, None, :] * per_assign, axis=2)
        grad_rows = take_rows(by_expert(row_grad), slot_index).astype(jnp.float32).reshape(per_row, TOPK, D)
        token_grad = jnp.sum(grad_rows, axis=1).astype(jnp.bfloat16)
        new_totals = tuple(
            total_sum + lax.optimization_barrier(part_sum.astype(jnp.bfloat16)).astype(jnp.float32)
            for total_sum, part_sum in zip(totals, (part_gate, part_up, part_down)))
        return new_totals, (mixed_out, token_grad, gate_grad)

    inputs = (tokens.reshape(N_DP, per_row, D), cotangent.reshape(N_DP, per_row, D),
              expert_ids.reshape(N_DP, per_row, TOPK), gate_weights.reshape(N_DP, per_row, TOPK))
    start_sums = (jnp.zeros((EXPERTS, D, FF), jnp.float32), jnp.zeros((EXPERTS, D, FF), jnp.float32),
                  jnp.zeros((EXPERTS, FF, D), jnp.float32))
    sums_all, outputs = lax.scan(one_row, start_sums, inputs)
    mixed_out, token_grad, gate_grad = outputs
    slot_grad_gate = jnp.take(sums_all[0], partner, axis=0)
    slot_grad_up = jnp.take(sums_all[1], partner, axis=0)
    slot_grad_down = jnp.take(sums_all[2], partner, axis=0)
    return (mixed_out.reshape(TOKENS, D), token_grad.reshape(TOKENS, D), gate_grad.reshape(TOKENS, TOPK),
            slot_grad_gate, slot_grad_up, slot_grad_down)
```

```python
import functools

import jax
import jax.numpy as jnp
from jax import lax
from jax.experimental import pallas as pl
from jax.experimental.pallas import tpu as pltpu
from jax.sharding import PartitionSpec as P

VMEM_BYTES = 48 * 1024 * 1024
F32 = jnp.float32
BF16 = jnp.bfloat16


def dot_nn(a, b):
    return lax.dot_general(a, b, (((1,), (0,)), ((), ())), preferred_element_type=F32)


def dot_nt(a, b):
    return lax.dot_general(a, b, (((1,), (1,)), ((), ())), preferred_element_type=F32)


def dot_tn(a, b):
    return lax.dot_general(a, b, (((0,), (0,)), ((), ())), preferred_element_type=F32)


def tile_of(size, want):
    while size % want:
        want //= 2
    return want


def params(**more):
    return pltpu.CompilerParams(vmem_limit_bytes=VMEM_BYTES, **more)


def whole(shape):
    return pl.BlockSpec(shape, lambda *_: (0,) * len(shape))


def cost(flops, nbytes):
    return pl.CostEstimate(flops=int(flops), bytes_accessed=int(nbytes), transcendentals=0)


def slots_of(ids, cap, me):
    rows, top = ids.shape
    block = jnp.bitwise_xor(ids, me)
    lane = lax.broadcasted_iota(jnp.int32, (rows, 128), 1)
    named = [(block[:, k : k + 1] == lane).astype(F32) for k in range(top)]
    strict = lax.broadcasted_iota(jnp.int32, (rows, rows), 0) > lax.broadcasted_iota(
        jnp.int32, (rows, rows), 1
    )
    before = dot_nn(strict.astype(BF16), sum(named).astype(BF16))
    slots = []
    for k in range(top):
        pos = jnp.sum(before * named[k], axis=1, keepdims=True).astype(jnp.int32)
        slots.append(block[:, k : k + 1] * cap + pos)
        before = before + named[k]
    return slots


def places_of(slots, total):
    rows = slots[0].shape[0]
    lane = lax.broadcasted_iota(jnp.int32, (rows, total), 1)
    return [(slot == lane).astype(BF16) for slot in slots]


def place_tokens(cap, me_ref, ids_ref, tok_ref, *outs):
    picks = places_of(slots_of(ids_ref[...], cap, me_ref[0]), cap * len(outs))
    rows = dot_tn(sum(picks), tok_ref[...])
    for b, out in enumerate(outs):
        out[...] = rows[b * cap : (b + 1) * cap].astype(BF16)


def place_grads(cap, me_ref, ids_ref, gates_ref, cot_ref, *outs):
    picks = places_of(slots_of(ids_ref[...], cap, me_ref[0]), cap * len(outs))
    cot = cot_ref[...].astype(F32)
    gates = gates_ref[...]
    rows = sum(
        dot_tn(pick, (gates[:, k : k + 1] * cot).astype(BF16)) for k, pick in enumerate(picks)
    )
    for b, out in enumerate(outs):
        out[...] = rows[b * cap : (b + 1) * cap].astype(BF16)


def forward(cap, groups, *refs):
    blocks, (gate_ref, up_ref), (x_ref, pre_ref, act_ref) = refs[:groups], refs[groups:-3], refs[-3:]

    @pl.when(pl.program_id(0) == 0)
    def _():
        x_ref[...] = jnp.concatenate([block[...] for block in blocks], axis=0)

    x = x_ref[...]
    gate_pre = dot_nn(x, gate_ref[0])
    up_pre = dot_nn(x, up_ref[0])
    pre_ref[0] = gate_pre
    pre_ref[1] = up_pre
    act_ref[...] = (gate_pre * jax.nn.sigmoid(gate_pre) * up_pre).astype(BF16)


def backward(cap, groups, *refs):
    blocks, (down_ref, pre_ref), (c_ref, grad_ref) = refs[:groups], refs[groups:-2], refs[-2:]

    @pl.when(pl.program_id(0) == 0)
    def _():
        c_ref[...] = jnp.concatenate([block[...] for block in blocks], axis=0)

    hidden_grad = dot_nt(c_ref[...], down_ref[0])
    gate_pre, up_pre = pre_ref[0], pre_ref[1]
    s = jax.nn.sigmoid(gate_pre)
    grad_ref[0] = (hidden_grad * up_pre * s * (1.0 + gate_pre * (1.0 - s))).astype(BF16)
    grad_ref[1] = (hidden_grad * gate_pre * s).astype(BF16)


def expert_rows(cap, act_ref, down_ref, *outs):
    rows = dot_nn(act_ref[...], down_ref[0])
    for b, out in enumerate(outs):
        out[...] = rows[b * cap : (b + 1) * cap].astype(BF16)


def input_rows(cap, grad_ref, gate_ref, up_ref, *outs):
    rows = dot_nt(grad_ref[0], gate_ref[0]) + dot_nt(grad_ref[1], up_ref[0])
    for b, out in enumerate(outs):
        out[...] = rows[b * cap : (b + 1) * cap].astype(BF16)


def both(own_ref, other_ref, *at):
    if at:
        return jnp.concatenate([own_ref[at[0]], other_ref[at[0]]], axis=0)
    return jnp.concatenate([own_ref[...], other_ref[...]], axis=0)


def down_share(core_ref, act_own, act_other, c_own, c_other, out_ref, turned):
    @pl.when(pl.program_id(0) == 0)
    def _():
        turned[...] = both(act_own, act_other).T

    out_ref[0] = dot_nn(turned[...], both(c_own, c_other)).astype(BF16)


def gate_up_share(core_ref, x_own, x_other, g_own, g_other, gate_ref, up_ref):
    turned = both(x_own, x_other).T
    gate_ref[0] = dot_nn(turned, both(g_own, g_other, 0)).astype(BF16)
    up_ref[0] = dot_nn(turned, both(g_own, g_other, 1)).astype(BF16)


def combine(cap, groups, me_ref, ids_ref, gates_ref, cot_ref, *refs):
    outs, grads = refs[:groups], refs[groups : 2 * groups]
    mixed_ref, token_ref, dots_ref = refs[2 * groups :]
    picks = places_of(slots_of(ids_ref[...], cap, me_ref[0]), cap * groups)
    gates = gates_ref[...]
    width = mixed_ref.shape[1]
    tile = tile_of(width, 512)
    dots = [0.0] * len(picks)
    for start in range(0, width, tile):
        cols = slice(start, start + tile)
        rows = jnp.concatenate([ref[:, cols] for ref in outs], axis=0)
        cot = cot_ref[:, cols].astype(F32)
        mixed = 0.0
        for k, pick in enumerate(picks):
            picked = dot_nn(pick, rows)
            mixed = mixed + gates[:, k : k + 1] * picked
            dots[k] = dots[k] + jnp.sum(cot * picked, axis=1, keepdims=True)
        mixed_ref[:, cols] = mixed.astype(BF16)
        rows = jnp.concatenate([ref[:, cols] for ref in grads], axis=0)
        token_ref[:, cols] = dot_nn(sum(picks), rows).astype(BF16)
    dots_ref[...] = jnp.concatenate(dots, axis=1)


def share_kernels(core, chips, cols, act, act_other, c_rows, c_other, x_rows, x_other, grads, grads_other):
    total, width = x_rows.shape
    ff = act.shape[1]
    core_arr = core.astype(jnp.int32).reshape(1)

    def mine(z, core_ref):
        return (0, 2 * z + core_ref[0])

    down_q = pl.pallas_call(
        down_share,
        out_shape=jax.ShapeDtypeStruct((chips, ff, cols), BF16),
        grid_spec=pltpu.PrefetchScalarGridSpec(
            num_scalar_prefetch=1,
            grid=(chips,),
            in_specs=[whole((total, ff))] * 2 + [pl.BlockSpec((total, cols), mine)] * 2,
            out_specs=pl.BlockSpec((1, ff, cols), lambda z, _: (z, 0, 0)),
            scratch_shapes=[pltpu.VMEM((ff, 2 * total), BF16)],
        ),
        compiler_params=params(),
        cost_estimate=cost(2 * total * width * ff, 7e6),
        name="down_share",
    )(core_arr, act, act_other, c_rows, c_other)
    gate_q, up_q = pl.pallas_call(
        gate_up_share,
        out_shape=[jax.ShapeDtypeStruct((chips, cols, ff), BF16)] * 2,
        grid_spec=pltpu.PrefetchScalarGridSpec(
            num_scalar_prefetch=1,
            grid=(chips,),
            in_specs=[pl.BlockSpec((total, cols), mine)] * 2 + [whole((2, total, ff))] * 2,
            out_specs=[pl.BlockSpec((1, cols, ff), lambda z, _: (z, 0, 0))] * 2,
        ),
        compiler_params=params(),
        cost_estimate=cost(4 * total * width * ff, 9e6),
        name="gate_up_share",
    )(core_arr, x_rows, x_other, grads, grads_other)
    return down_q, gate_q, up_q


def share_dots(core, chips, cols, act, act_other, c_rows, c_other, x_rows, x_other, grads, grads_other):
    def mine(own, other):
        rows = jnp.concatenate([own, other], axis=0).reshape(-1, chips, 2, cols)
        return lax.dynamic_index_in_dim(rows, core, 2, keepdims=False)

    def dot(left, right, spec):
        return jnp.einsum(spec, left, right, preferred_element_type=F32).astype(BF16)

    acts = jnp.concatenate([act, act_other], axis=0)
    both_grads = jnp.concatenate([grads, grads_other], axis=1)
    x = mine(x_rows, x_other)
    return (
        dot(acts, mine(c_rows, c_other), "rf,rzc->zfc"),
        dot(x, both_grads[0], "rzc,rf->zcf"),
        dot(x, both_grads[1], "rzc,rf->zcf"),
    )


def line_sums(shares, chips, chip):
    up = [[(2 * i + c, 2 * i + 2 + c) for i in range(min(s, chips - 1)) for c in (0, 1)] for s in range(1, chips)]
    down = [[(2 * (chips - 1) - a + 2 * (a % 2), 2 * (chips - 1) - b + 2 * (b % 2)) for a, b in step] for step in up]

    def share_at(share, index):
        return lax.dynamic_index_in_dim(share, jnp.clip(index, 0, chips - 1), 0, keepdims=False)

    def add(part, own):
        return (part.astype(F32) + own.astype(F32)).astype(BF16)

    state = [[None, None] for _ in shares]
    for s in range(1, chips):
        for n, share in enumerate(shares):
            for side, index in ((0, chips - s + chip), (1, chip - chips + s)):
                message = share_at(share, index)
                if state[n][side] is not None:
                    message = add(state[n][side], message)
                state[n][side] = lax.ppermute(message, "dp", (up, down)[side][s - 1])
    totals = []
    for n, share in enumerate(shares):
        own = share_at(share, chip).astype(F32)
        for side in state[n]:
            if side is not None:
                own = own + side.astype(F32)
        totals.append(own.astype(BF16))
    return totals


def relocated(total, partner, me, groups):
    if groups == 4:
        turn = jnp.bitwise_xor(lax.dynamic_index_in_dim(partner, me, 0, keepdims=False), me)
        first = lax.ppermute(total, "expert", [(i, i ^ 1) for i in range(groups)])
        second = lax.ppermute(
            jnp.where(turn == 3, first, total), "expert", [(i, i ^ 2) for i in range(groups)]
        )
        return jnp.where(turn == 1, first, second).astype(F32)[None]
    is_mate = (partner == me)[:, None, None]
    parts = jnp.where(is_mate, total[None], jnp.zeros_like(total)[None])
    parts = lax.all_to_all(parts, "expert", split_axis=0, concat_axis=0, tiled=True)
    mate = lax.dynamic_index_in_dim(partner, me, 0, keepdims=False)
    return lax.dynamic_index_in_dim(parts, mate, 0, keepdims=True).astype(F32)


def shards(tokens, cotangent, expert_ids, gate_weights, partner, w_gate, w_up, w_down):
    groups = lax.axis_size("expert")
    replicas = lax.axis_size("dp")
    me = lax.axis_index("expert")
    replica = lax.axis_index("dp")
    chips, chip, core = replicas // 2, replica // 2, replica % 2
    count, width = tokens.shape
    top = expert_ids.shape[1]
    ff = w_gate.shape[2]
    cap = min(count, 5 * count * top // (4 * groups))
    total = groups * cap
    cols = width // replicas
    me_arr = me.astype(jnp.int32).reshape(1)
    smem = pl.BlockSpec(memory_space=pltpu.SMEM)
    vmem = pl.BlockSpec(memory_space=pltpu.VMEM)
    block_shape = jax.ShapeDtypeStruct((cap, width), BF16)

    def exchange(blocks):
        return [blocks[0]] + [
            lax.ppermute(blocks[b], "expert", [(i, i ^ b) for i in range(groups)])
            for b in range(1, groups)
        ]

    def swap(part):
        return lax.ppermute(part, "dp", [(i, i ^ 1) for i in range(replicas)])

    x_blocks = pl.pallas_call(
        functools.partial(place_tokens, cap),
        out_shape=[block_shape] * groups,
        in_specs=[smem, vmem, vmem],
        out_specs=[vmem] * groups,
        compiler_params=params(),
        name="place_tokens",
    )(me_arr, expert_ids, tokens)
    c_blocks = pl.pallas_call(
        functools.partial(place_grads, cap),
        out_shape=[block_shape] * groups,
        in_specs=[smem, vmem, vmem, vmem],
        out_specs=[vmem] * groups,
        compiler_params=params(),
        name="place_grads",
    )(me_arr, expert_ids, gate_weights, cotangent)
    x_blocks = exchange(x_blocks)
    *c_blocks, x_blocks = lax.optimization_barrier((*c_blocks, x_blocks))
    c_blocks = exchange(c_blocks)

    tile = tile_of(ff, 256)
    x_rows, pre, act = pl.pallas_call(
        functools.partial(forward, cap, groups),
        out_shape=[
            jax.ShapeDtypeStruct((total, width), BF16),
            jax.ShapeDtypeStruct((2, total, ff), F32),
            jax.ShapeDtypeStruct((total, ff), BF16),
        ],
        grid=(ff // tile,),
        in_specs=[whole((cap, width))] * groups
        + [pl.BlockSpec((1, width, tile), lambda j: (0, 0, j))] * 2,
        out_specs=[
            whole((total, width)),
            pl.BlockSpec((2, total, tile), lambda j: (0, 0, j)),
            pl.BlockSpec((total, tile), lambda j: (0, j)),
        ],
        compiler_params=params(),
        cost_estimate=cost(4 * total * width * ff, 10e6),
        name="forward",
    )(*x_blocks, w_gate, w_up)

    c_rows, grads = pl.pallas_call(
        functools.partial(backward, cap, groups),
        out_shape=[
            jax.ShapeDtypeStruct((total, width), BF16),
            jax.ShapeDtypeStruct((2, total, ff), BF16),
        ],
        grid=(ff // tile,),
        in_specs=[whole((cap, width))] * groups
        + [
            pl.BlockSpec((1, tile, width), lambda j: (0, j, 0)),
            pl.BlockSpec((2, total, tile), lambda j: (0, 0, j)),
        ],
        out_specs=[
            whole((total, width)),
            pl.BlockSpec((2, total, tile), lambda j: (0, 0, j)),
        ],
        compiler_params=params(),
        cost_estimate=cost(2 * total * width * ff, 10e6),
        name="backward",
    )(*c_blocks, w_down, pre)

    act_other, c_other, x_other, grads_other = swap(act), swap(c_rows), swap(x_rows), swap(grads)

    if cols % 128 == 0:
        down_q, gate_q, up_q = share_kernels(
            core, chips, cols, act, act_other, c_rows, c_other, x_rows, x_other, grads, grads_other
        )
    else:
        down_q, gate_q, up_q = share_dots(
            core, chips, cols, act, act_other, c_rows, c_other, x_rows, x_other, grads, grads_other
        )

    wide = tile_of(width, 512)
    out_blocks = pl.pallas_call(
        functools.partial(expert_rows, cap),
        out_shape=[block_shape] * groups,
        grid=(width // wide,),
        in_specs=[whole((total, ff)), pl.BlockSpec((1, ff, wide), lambda j: (0, 0, j))],
        out_specs=[pl.BlockSpec((cap, wide), lambda j: (0, j))] * groups,
        compiler_params=params(),
        cost_estimate=cost(2 * total * width * ff, 5e6),
        name="expert_rows",
    )(act, w_down)
    grad_blocks = pl.pallas_call(
        functools.partial(input_rows, cap),
        out_shape=[block_shape] * groups,
        grid=(width // wide,),
        in_specs=[whole((2, total, ff))] + [pl.BlockSpec((1, wide, ff), lambda j: (0, j, 0))] * 2,
        out_specs=[pl.BlockSpec((cap, wide), lambda j: (0, j))] * groups,
        compiler_params=params(),
        cost_estimate=cost(4 * total * width * ff, 9e6),
        name="input_rows",
    )(grads, w_gate, w_up)
    out_blocks = exchange(out_blocks)
    grad_blocks = exchange(grad_blocks)

    sums = line_sums([down_q, gate_q, up_q], chips, chip)
    slot_down, slot_gate, slot_up = [relocated(part, partner, me, groups) for part in sums]

    mixed_out, token_grad, gate_grad = pl.pallas_call(
        functools.partial(combine, cap, groups),
        out_shape=[
            jax.ShapeDtypeStruct((count, width), BF16),
            jax.ShapeDtypeStruct((count, width), BF16),
            jax.ShapeDtypeStruct((count, top), F32),
        ],
        in_specs=[smem] + [vmem] * (3 + 2 * groups),
        out_specs=[vmem] * 3,
        compiler_params=params(),
        cost_estimate=cost(6 * total * width * count, 6e6),
        name="combine",
    )(me_arr, expert_ids, gate_weights, cotangent, *out_blocks, *grad_blocks)
    return mixed_out, token_grad, gate_grad, slot_gate, slot_up, slot_down


def solution(mesh):
    rows = P(("dp", "expert"), None)
    in_specs = (
        rows,
        rows,
        rows,
        rows,
        P(),
        P("expert", None, None),
        P("expert", None, None),
        P("expert", None, None),
    )
    out_specs = (
        rows,
        rows,
        rows,
        P("expert", "dp", None),
        P("expert", "dp", None),
        P("expert", None, "dp"),
    )
    return jax.shard_map(shards, mesh=mesh, in_specs=in_specs, out_specs=out_specs, check_vma=False)
```

```python
import functools

import jax
import jax.numpy as jnp
from jax import lax
from jax.experimental import pallas as pl
from jax.experimental.pallas import tpu as pltpu
from jax.sharding import PartitionSpec as P

VMEM_BYTES = 32 * 1024 * 1024
F32 = jnp.float32
BF16 = jnp.bfloat16


def dot_nn(a, b):
    return lax.dot_general(a, b, (((1,), (0,)), ((), ())), preferred_element_type=F32)


def dot_nt(a, b):
    return lax.dot_general(a, b, (((1,), (1,)), ((), ())), preferred_element_type=F32)


def dot_tn(a, b):
    return lax.dot_general(a, b, (((0,), (0,)), ((), ())), preferred_element_type=F32)


def tile_of(size, want):
    while size % want:
        want //= 2
    return want


def params(**more):
    return pltpu.CompilerParams(vmem_limit_bytes=VMEM_BYTES, **more)


def whole(shape):
    return pl.BlockSpec(shape, lambda *_: (0,) * len(shape))


def cost(flops, nbytes):
    return pl.CostEstimate(flops=1000, bytes_accessed=1000, transcendentals=0)


def picks_of(ids, cap, groups, me):
    top, count = ids.shape
    block = jnp.bitwise_xor(ids, me)
    lane = lax.broadcasted_iota(jnp.int32, (max(groups, 8), count), 0)
    named = [(block[k : k + 1] == lane).astype(F32) for k in range(top)]
    earlier = lax.broadcasted_iota(jnp.int32, (count, count), 0) < lax.broadcasted_iota(
        jnp.int32, (count, count), 1
    )
    before = dot_nn(sum(named).astype(BF16), earlier.astype(BF16))
    row = lax.broadcasted_iota(jnp.int32, (groups * cap, count), 0)
    picks = []
    for k in range(top):
        pos = jnp.sum(before * named[k], axis=0, keepdims=True).astype(jnp.int32)
        picks.append(block[k : k + 1] * cap + pos == row)
        before = before + named[k]
    return picks


def place_tokens(cap, groups, me_ref, ids_ref, tok_ref, *outs):
    picks = picks_of(ids_ref[...], cap, groups, me_ref[0])
    rows = dot_nn(sum(pick.astype(BF16) for pick in picks), tok_ref[...])
    for b, out in enumerate(outs):
        out[...] = rows[b * cap : (b + 1) * cap].astype(BF16)


def place_grads(cap, groups, me_ref, ids_ref, gates_ref, cot_ref, *outs):
    picks = picks_of(ids_ref[...], cap, groups, me_ref[0])
    gates = gates_ref[...]
    weight = sum(
        jnp.sum(jnp.where(pick, gates[k : k + 1], 0.0), axis=1, keepdims=True)
        for k, pick in enumerate(picks)
    )
    rows = dot_nn(sum(pick.astype(BF16) for pick in picks), cot_ref[...])
    rows = (rows * weight).astype(BF16)
    for b, out in enumerate(outs):
        out[...] = rows[b * cap : (b + 1) * cap]


def forward(cap, groups, *refs):
    blocks, (gate_ref, up_ref), (x_ref, pre_ref, act_ref) = refs[:groups], refs[groups:-3], refs[-3:]

    @pl.when(pl.program_id(0) == 0)
    def _():
        x_ref[...] = jnp.concatenate([block[...] for block in blocks], axis=0)

    x = x_ref[...]
    gate_pre = dot_nn(x, gate_ref[0])
    up_pre = dot_nn(x, up_ref[0])
    pre_ref[0] = gate_pre
    pre_ref[1] = up_pre
    act_ref[...] = (gate_pre * jax.nn.sigmoid(gate_pre) * up_pre).astype(BF16)


def backward(c_ref, down_ref, pre_ref, grad_ref):
    hidden_grad = dot_nt(c_ref[...], down_ref[0])
    gate_pre, up_pre = pre_ref[0], pre_ref[1]
    s = jax.nn.sigmoid(gate_pre)
    grad_ref[0] = (hidden_grad * up_pre * s * (1.0 + gate_pre * (1.0 - s))).astype(BF16)
    grad_ref[1] = (hidden_grad * gate_pre * s).astype(BF16)


def join(*refs):
    blocks, out_ref = refs[:-1], refs[-1]
    out_ref[...] = jnp.concatenate([block[...] for block in blocks], axis=0)


def expert_rows(cap, act_ref, down_ref, *outs):
    rows = dot_nn(act_ref[...], down_ref[0])
    for b, out in enumerate(outs):
        out[...] = rows[b * cap : (b + 1) * cap].astype(BF16)


def input_rows(cap, grad_ref, gate_ref, up_ref, *outs):
    rows = dot_nt(grad_ref[0], gate_ref[0]) + dot_nt(grad_ref[1], up_ref[0])
    for b, out in enumerate(outs):
        out[...] = rows[b * cap : (b + 1) * cap].astype(BF16)


def both(own_ref, other_ref, *at):
    if at:
        return jnp.concatenate([own_ref[at[0]], other_ref[at[0]]], axis=0)
    return jnp.concatenate([own_ref[...], other_ref[...]], axis=0)


def store_at_step(outs, value):
    for n, out in enumerate(outs):

        @pl.when(pl.program_id(0) == n)
        def _(out=out):
            out[...] = value


def down_share(order_ref, act_own, act_other, c_own, c_other, *outs_and_scratch):
    *outs, turned = outs_and_scratch

    @pl.when(pl.program_id(0) == 0)
    def _():
        turned[...] = both(act_own, act_other).T

    store_at_step(outs, dot_nn(turned[...], both(c_own, c_other)).astype(BF16))


def gate_up_share(order_ref, x_own, x_other, g_own, g_other, *outs):
    half = len(outs) // 2
    turned = both(x_own, x_other).T
    store_at_step(outs[:half], dot_nn(turned, both(g_own, g_other, 0)).astype(BF16))
    store_at_step(outs[half:], dot_nn(turned, both(g_own, g_other, 1)).astype(BF16))


def add_kernel(left_ref, right_ref, out_ref):
    out_ref[...] = (left_ref[...].astype(F32) + right_ref[...].astype(F32)).astype(out_ref.dtype)


def added(name, dtype, left, right):
    return pl.pallas_call(
        add_kernel,
        out_shape=jax.ShapeDtypeStruct(left.shape, dtype),
        compiler_params=params(),
        cost_estimate=cost(0, 0),
        name=name,
    )(left, right)


def end_kernel(end_ref, alone_ref, left_ref, right_ref, out_ref):
    @pl.when(end_ref[0] == 1)
    def _():
        out_ref[...] = alone_ref[...]

    @pl.when(end_ref[0] == 0)
    def _():
        out_ref[...] = (left_ref[...].astype(F32) + right_ref[...].astype(F32)).astype(BF16)


def at_end(kernel, name, end, *parts):
    smem, vmem = pl.BlockSpec(memory_space=pltpu.SMEM), pl.BlockSpec(memory_space=pltpu.VMEM)
    return pl.pallas_call(
        kernel,
        out_shape=jax.ShapeDtypeStruct(parts[0].shape, BF16),
        in_specs=[smem] + [vmem] * len(parts),
        out_specs=vmem,
        compiler_params=params(),
        cost_estimate=cost(0, 0),
        name=name,
    )(end, *parts)


def final_kernel(end_ref, near_ref, last_ref, inner_ref, middle_ref, out_ref):
    last = last_ref[...].astype(F32)

    @pl.when(end_ref[0] == 1)
    def _():
        out_ref[...] = (near_ref[...].astype(F32) + last).astype(BF16)

    @pl.when(end_ref[0] == 0)
    def _():
        inner = inner_ref[...].astype(F32) + middle_ref[...].astype(F32)
        out_ref[...] = (inner + last).astype(BF16)


def combine(cap, groups, me_ref, ids_ref, gates_ref, cot_ref, *refs):
    outs, grads = refs[:groups], refs[groups : 2 * groups]
    mixed_ref, token_ref, dots_ref = refs[2 * groups :]
    picks = [pick.astype(BF16) for pick in picks_of(ids_ref[...], cap, groups, me_ref[0])]
    gates = gates_ref[...]
    count, width = mixed_ref.shape
    eye = lax.broadcasted_iota(jnp.int32, (count, count), 0) == lax.broadcasted_iota(
        jnp.int32, (count, count), 1
    )
    weights = [
        jnp.sum(jnp.where(eye, gates[k : k + 1], 0.0), axis=1, keepdims=True)
        for k in range(len(picks))
    ]
    tile = tile_of(width, 512)
    dots = [0.0] * len(picks)
    for start in range(0, width, tile):
        cols = slice(start, start + tile)
        rows = jnp.concatenate([ref[:, cols] for ref in outs], axis=0)
        cot = cot_ref[:, cols].astype(F32)
        mixed = 0.0
        for k, pick in enumerate(picks):
            picked = dot_tn(pick, rows)
            mixed = mixed + weights[k] * picked
            dots[k] = dots[k] + jnp.sum(cot * picked, axis=1, keepdims=True)
        mixed_ref[:, cols] = mixed.astype(BF16)
        rows = jnp.concatenate([ref[:, cols] for ref in grads], axis=0)
        token_ref[:, cols] = dot_tn(sum(picks), rows).astype(BF16)
    dots_ref[...] = jnp.concatenate(
        [jnp.sum(jnp.where(eye, dot, 0.0), axis=0, keepdims=True) for dot in dots], axis=0
    )


def after(value, *others):
    return lax.optimization_barrier((value, others))[0]


def rows_of_core(core, count, cols, own, other):
    rows = jnp.concatenate([own, other], axis=0).reshape(-1, count, 2, cols)
    return lax.dynamic_index_in_dim(rows, core, 2, keepdims=False)


def down_shares(order, cols, name, act, act_other, c_rows, c_other):
    total, ff = act.shape
    count = order.shape[0]
    block = pl.BlockSpec((total, cols), lambda n, order_ref: (0, order_ref[n]))
    return pl.pallas_call(
        down_share,
        out_shape=[jax.ShapeDtypeStruct((ff, cols), BF16)] * count,
        grid_spec=pltpu.PrefetchScalarGridSpec(
            num_scalar_prefetch=1,
            grid=(count,),
            in_specs=[whole((total, ff))] * 2 + [block] * 2,
            out_specs=[whole((ff, cols))] * count,
            scratch_shapes=[pltpu.VMEM((ff, 2 * total), BF16)],
        ),
        compiler_params=params(),
        cost_estimate=cost(4 * total * count * cols * ff, 5e6),
        name=name,
    )(order, act, act_other, c_rows, c_other)


def gate_up_shares(order, cols, name, x_rows, x_other, grads, grads_other):
    total, width = x_rows.shape
    ff = grads.shape[2]
    count = order.shape[0]
    block = pl.BlockSpec((total, cols), lambda n, order_ref: (0, order_ref[n]))
    return pl.pallas_call(
        gate_up_share,
        out_shape=[jax.ShapeDtypeStruct((cols, ff), BF16)] * (2 * count),
        grid_spec=pltpu.PrefetchScalarGridSpec(
            num_scalar_prefetch=1,
            grid=(count,),
            in_specs=[block] * 2 + [whole((2, total, ff))] * 2,
            out_specs=[whole((cols, ff))] * (2 * count),
        ),
        compiler_params=params(),
        cost_estimate=cost(8 * total * count * cols * ff, 6e6),
        name=name,
    )(order, x_rows, x_other, grads, grads_other)


def add(part, own):
    return (part.astype(F32) + own.astype(F32)).astype(BF16)


class LineSum:
    def __init__(self, share, chips, chip):
        self.share, self.chips, self.chip = share, chips, chip
        self.got = None
        self.steps = 0

    def share_at(self, index):
        index = jnp.clip(index, 0, self.chips - 1)
        return lax.dynamic_index_in_dim(self.share, index, 0, keepdims=False)

    def pairs(self, s):
        last = self.chips - 1
        up = [(i, i + 1) for i in range(s)]
        down = [(last - a, last - b) for a, b in up]
        return [[(2 * a + c, 2 * b + c) for a, b in way for c in (0, 1)] for way in (up, down)]

    def message(self, index, side):
        own = self.share_at(index)
        return own if self.got is None else add(self.got[side], own)

    def step(self):
        self.steps += 1
        s, chip, chips = self.steps, self.chip, self.chips
        up, down = self.pairs(s)
        if 2 * s < chips - 1:
            index = jnp.where(chip < s, chips - s + chip, chip - chips + s)
            sent = lax.ppermute(self.message(index, 0), "dp", up + down)
            self.got = (sent, sent)
        else:
            self.got = (
                lax.ppermute(self.message(chips - s + chip, 0), "dp", up),
                lax.ppermute(self.message(chip - chips + s, 1), "dp", down),
            )

    def total(self):
        own = self.share_at(self.chip).astype(F32)
        return (own + self.got[0].astype(F32) + self.got[1].astype(F32)).astype(BF16)


def relocated(total, turn, partner, me, groups):
    if turn is not None:
        return lax.ppermute(total, "expert", [(i, i ^ turn) for i in range(groups)]).astype(F32)[None]
    is_mate = (partner == me)[:, None, None]
    parts = jnp.where(is_mate, total[None], jnp.zeros_like(total)[None])
    parts = lax.all_to_all(parts, "expert", split_axis=0, concat_axis=0, tiled=True)
    mate = lax.dynamic_index_in_dim(partner, me, 0, keepdims=False)
    return lax.dynamic_index_in_dim(parts, mate, 0, keepdims=True).astype(F32)


def shards(tokens, cotangent, expert_ids, gate_weights, partner, w_gate, w_up, w_down):
    args = (tokens, cotangent, expert_ids.T, gate_weights.T, partner, w_gate, w_up, w_down)
    if lax.axis_size("expert") == 4:
        turns = [functools.partial(layer, turn) for turn in (1, 2, 3)]
        return lax.switch(partner[0] - 1, turns, *args)
    return layer(None, *args)


def layer(turn, tokens, cotangent, ids, gates, partner, w_gate, w_up, w_down):
    groups = lax.axis_size("expert")
    replicas = lax.axis_size("dp")
    me = lax.axis_index("expert")
    replica = lax.axis_index("dp")
    chips, chip, core = replicas // 2, replica // 2, replica % 2
    count, width = tokens.shape
    top = ids.shape[0]
    ff = w_gate.shape[2]
    cap = min(count, 5 * count * top // (4 * groups))
    total = groups * cap
    cols = width // replicas
    me_arr = me.astype(jnp.int32).reshape(1)
    smem = pl.BlockSpec(memory_space=pltpu.SMEM)
    vmem = pl.BlockSpec(memory_space=pltpu.VMEM)
    block_shape = jax.ShapeDtypeStruct((cap, width), BF16)

    def exchange(blocks):
        return [blocks[0]] + [
            lax.ppermute(blocks[b], "expert", [(i, i ^ b) for i in range(groups)])
            for b in range(1, groups)
        ]

    def swap(part):
        return lax.ppermute(part, "dp", [(i, i ^ 1) for i in range(replicas)])

    def joined(blocks, name):
        return pl.pallas_call(
            join,
            out_shape=jax.ShapeDtypeStruct((total, blocks[0].shape[1]), BF16),
            in_specs=[vmem] * groups,
            out_specs=vmem,
            compiler_params=params(),
            cost_estimate=cost(0, 4 * total * blocks[0].shape[1]),
            name=name,
        )(*blocks)

    x_blocks = pl.pallas_call(
        functools.partial(place_tokens, cap, groups),
        out_shape=[block_shape] * groups,
        in_specs=[smem, vmem, vmem],
        out_specs=[vmem] * groups,
        compiler_params=params(),
        name="place_tokens",
    )(me_arr, ids, tokens)
    c_blocks = pl.pallas_call(
        functools.partial(place_grads, cap, groups),
        out_shape=[block_shape] * groups,
        in_specs=[smem, vmem, vmem, vmem],
        out_specs=[vmem] * groups,
        compiler_params=params(),
        name="place_grads",
    )(me_arr, ids, gates, cotangent)
    x_blocks = exchange(x_blocks)
    c_blocks = exchange(c_blocks)

    tile = tile_of(ff, 256)
    x_rows, pre, act = pl.pallas_call(
        functools.partial(forward, cap, groups),
        out_shape=[
            jax.ShapeDtypeStruct((total, width), BF16),
            jax.ShapeDtypeStruct((2, total, ff), F32),
            jax.ShapeDtypeStruct((total, ff), BF16),
        ],
        grid=(ff // tile,),
        in_specs=[whole((cap, width))] * groups
        + [pl.BlockSpec((1, width, tile), lambda j: (0, 0, j))] * 2,
        out_specs=[
            whole((total, width)),
            pl.BlockSpec((2, total, tile), lambda j: (0, 0, j)),
            pl.BlockSpec((total, tile), lambda j: (0, j)),
        ],
        compiler_params=params(),
        cost_estimate=cost(4 * total * width * ff, 10e6),
        name="forward",
    )(*x_blocks, w_gate, w_up)
    act_other = swap(act)

    wide = tile_of(width, 512)

    def run_backward(c_rows):
        return pl.pallas_call(
            backward,
            out_shape=jax.ShapeDtypeStruct((2, total, ff), BF16),
            grid=(ff // tile,),
            in_specs=[
                whole((total, width)),
                pl.BlockSpec((1, tile, width), lambda j: (0, j, 0)),
                pl.BlockSpec((2, total, tile), lambda j: (0, 0, j)),
            ],
            out_specs=pl.BlockSpec((2, total, tile), lambda j: (0, 0, j)),
            compiler_params=params(),
            cost_estimate=cost(2 * total * width * ff, 10e6),
            name="backward",
        )(c_rows, w_down, pre)

    def run_expert_rows(act):
        return pl.pallas_call(
            functools.partial(expert_rows, cap),
            out_shape=[block_shape] * groups,
            grid=(width // wide,),
            in_specs=[whole((total, ff)), pl.BlockSpec((1, ff, wide), lambda j: (0, 0, j))],
            out_specs=[pl.BlockSpec((cap, wide), lambda j: (0, j))] * groups,
            compiler_params=params(),
            cost_estimate=cost(2 * total * width * ff, 5e6),
            name="expert_rows",
        )(act, w_down)

    def run_input_rows(grads):
        return pl.pallas_call(
            functools.partial(input_rows, cap),
            out_shape=[block_shape] * groups,
            grid=(width // wide,),
            in_specs=[whole((2, total, ff))] + [pl.BlockSpec((1, wide, ff), lambda j: (0, j, 0))] * 2,
            out_specs=[pl.BlockSpec((cap, wide), lambda j: (0, j))] * groups,
            compiler_params=params(),
            cost_estimate=cost(4 * total * width * ff, 9e6),
            name="input_rows",
        )(grads, w_gate, w_up)

    if turn is not None and chips == 4 and cols % 128 == 0:
        low = chip < 2
        end = ((chip == 0) | (chip == 3)).astype(jnp.int32).reshape(1)
        order = (2 * jnp.where(low, 3 - jnp.arange(4), jnp.arange(4)) + core).astype(jnp.int32)

        def swap_ends(part):
            return lax.ppermute(part, "dp", [(i, i ^ 2) for i in range(replicas)])

        def swap_middle(part):
            pairs = [(2, 4), (4, 2), (3, 5), (5, 3), (0, 1), (1, 0), (6, 7), (7, 6)]
            return lax.ppermute(part, "dp", pairs)

        def to_mate(part):
            return lax.ppermute(part, "expert", [(i, i ^ turn) for i in range(groups)])

        c_rows = joined(after(c_blocks, act), "join_grads")
        c_other, x_other = swap(c_rows), swap(x_rows)
        grads = run_backward(c_rows)
        d_a, d_b, d_c, d_d = down_shares(
            order, cols, "down_shares", act, act_other, c_rows, after(c_other, grads)
        )
        d_1, d_2 = swap_ends(d_a), swap_ends(after(d_b, d_a))
        grads_other = swap(after(grads, d_a))

        out_rows = run_expert_rows(after(act, d_a))
        out_blocks = exchange(out_rows)
        g_a, g_b, u_a, u_b = gate_up_shares(
            order[:2], cols, "gate_up_far", x_rows, x_other, grads, after(grads_other, *out_rows)
        )

        m = added("down_mid1", BF16, *after((d_1, d_a), g_a))
        d_m1, g_1 = swap_middle(m), swap_ends(after(g_a, m))
        grad_rows = run_input_rows(after(grads, m))
        grad_blocks = exchange(grad_rows)

        m = added("down_mid2", BF16, *after((d_2, d_b), *grad_rows))
        d_m2, u_1 = swap_middle(m), swap_ends(after(u_a, m))
        g_c, g_d, u_c, u_d = gate_up_shares(
            order[2:], cols, "gate_up_near", x_rows, x_other, grads, after(grads_other, m)
        )

        m = added("gate_mid1", BF16, *after((g_1, g_a), g_c))
        g_m1 = swap_middle(m)
        e = at_end(end_kernel, "down_last", end, *after((d_c, d_m1, d_d), m, *out_blocks))
        d_3 = swap_ends(e)
        m = added("up_mid1", BF16, *after((u_1, u_a), e))
        u_m1, g_2 = swap_middle(m), swap_ends(after(g_b, m))

        t = at_end(final_kernel, "down_sum", end, *after((d_d, d_3, d_c, d_m2), m, *grad_blocks))
        d_t, u_2 = to_mate(t), swap_ends(after(u_b, t))
        m = added("gate_mid2", BF16, *after((g_2, g_b), t))
        g_m2 = swap_middle(m)
        e = at_end(end_kernel, "gate_last", end, *after((g_c, g_m1, g_d), m))
        g_3 = swap_ends(e)
        m = added("up_mid2", BF16, *after((u_2, u_b), e))
        u_m2 = swap_middle(m)
        e = at_end(end_kernel, "up_last", end, *after((u_c, u_m1, u_d), m))
        u_3 = swap_ends(e)
        t = at_end(final_kernel, "gate_sum", end, *after((g_d, g_3, g_c, g_m2), e))
        g_t = to_mate(t)
        t = at_end(final_kernel, "up_sum", end, *after((u_d, u_3, u_c, u_m2), t))
        u_t = to_mate(t)
        slot_down, slot_gate, slot_up = [part.astype(F32)[None] for part in (d_t, g_t, u_t)]
    else:
        c_rows = joined(c_blocks, "join_grads")
        grads = run_backward(c_rows)
        out_blocks = exchange(run_expert_rows(act))
        grad_blocks = exchange(run_input_rows(grads))
        acts = jnp.concatenate([act, act_other], axis=0)
        both_grads = jnp.concatenate([grads, swap(grads)], axis=1)
        c_both = rows_of_core(core, chips, cols, c_rows, swap(c_rows))
        x_both = rows_of_core(core, chips, cols, x_rows, swap(x_rows))

        def dot(spec, left, right):
            return jnp.einsum(spec, left, right, preferred_element_type=F32).astype(BF16)

        lines = [
            LineSum(share, chips, chip)
            for share in (
                dot("rf,rzc->zfc", acts, c_both),
                dot("rzc,rf->zcf", x_both, both_grads[0]),
                dot("rzc,rf->zcf", x_both, both_grads[1]),
            )
        ]
        for _ in range(1, chips):
            for line in lines:
                line.step()
        slot_down, slot_gate, slot_up = [
            relocated(line.total(), turn, partner, me, groups) for line in lines
        ]

    mixed_out, token_grad, gate_grad = pl.pallas_call(
        functools.partial(combine, cap, groups),
        out_shape=[
            jax.ShapeDtypeStruct((count, width), BF16),
            jax.ShapeDtypeStruct((count, width), BF16),
            jax.ShapeDtypeStruct((top, count), F32),
        ],
        in_specs=[smem] + [vmem] * (3 + 2 * groups),
        out_specs=[vmem] * 3,
        compiler_params=params(),
        cost_estimate=cost(6 * total * width * count, 6e6),
        name="combine",
    )(me_arr, ids, gates, cotangent, *out_blocks, *grad_blocks)
    return mixed_out, token_grad, gate_grad.T, slot_gate, slot_up, slot_down


def solution(mesh):
    rows = P(("dp", "expert"), None)
    in_specs = (
        rows,
        rows,
        rows,
        rows,
        P(),
        P("expert", None, None),
        P("expert", None, None),
        P("expert", None, None),
    )
    out_specs = (
        rows,
        rows,
        rows,
        P("expert", "dp", None),
        P("expert", "dp", None),
        P("expert", None, "dp"),
    )
    return jax.shard_map(shards, mesh=mesh, in_specs=in_specs, out_specs=out_specs, check_vma=False)
```

```python
import functools

import jax
import jax.numpy as jnp
from jax import lax
from jax.experimental import pallas as pl
from jax.experimental.pallas import tpu as pltpu
from jax.sharding import PartitionSpec as P

VMEM_BYTES = 48 * 1024 * 1024
F32 = jnp.float32
BF16 = jnp.bfloat16


def dot_nn(a, b):
    return lax.dot_general(a, b, (((1,), (0,)), ((), ())), preferred_element_type=F32)


def dot_nt(a, b):
    return lax.dot_general(a, b, (((1,), (1,)), ((), ())), preferred_element_type=F32)


def dot_tn(a, b):
    return lax.dot_general(a, b, (((0,), (0,)), ((), ())), preferred_element_type=F32)


def tile_of(size, want):
    while size % want:
        want //= 2
    return want


def params(**more):
    return pltpu.CompilerParams(vmem_limit_bytes=VMEM_BYTES, **more)


def whole(shape):
    return pl.BlockSpec(shape, lambda *_: (0,) * len(shape))


def cost(flops, nbytes):
    return pl.CostEstimate(flops=1000, bytes_accessed=1000, transcendentals=0)


def picks_of(ids, cap, groups, me):
    top, count = ids.shape
    block = jnp.bitwise_xor(ids, me)
    lane = lax.broadcasted_iota(jnp.int32, (max(groups, 8), count), 0)
    named = [(block[k : k + 1] == lane).astype(F32) for k in range(top)]
    earlier = lax.broadcasted_iota(jnp.int32, (count, count), 0) < lax.broadcasted_iota(
        jnp.int32, (count, count), 1
    )
    before = dot_nn(sum(named).astype(BF16), earlier.astype(BF16))
    row = lax.broadcasted_iota(jnp.int32, (groups * cap, count), 0)
    picks = []
    for k in range(top):
        pos = jnp.sum(before * named[k], axis=0, keepdims=True).astype(jnp.int32)
        picks.append(block[k : k + 1] * cap + pos == row)
        before = before + named[k]
    return picks


def place_tokens(cap, groups, me_ref, ids_ref, tok_ref, *outs):
    picks = picks_of(ids_ref[...], cap, groups, me_ref[0])
    rows = dot_nn(sum(pick.astype(BF16) for pick in picks), tok_ref[...])
    for b, out in enumerate(outs):
        out[...] = rows[b * cap : (b + 1) * cap].astype(BF16)


def place_grads(cap, groups, me_ref, ids_ref, gates_ref, cot_ref, *outs):
    picks = picks_of(ids_ref[...], cap, groups, me_ref[0])
    gates = gates_ref[...]
    weight = sum(
        jnp.sum(jnp.where(pick, gates[k : k + 1], 0.0), axis=1, keepdims=True)
        for k, pick in enumerate(picks)
    )
    rows = dot_nn(sum(pick.astype(BF16) for pick in picks), cot_ref[...])
    rows = (rows * weight).astype(BF16)
    for b, out in enumerate(outs):
        out[...] = rows[b * cap : (b + 1) * cap]


def forward(cap, groups, *refs):
    blocks, (gate_ref, up_ref), (x_ref, pre_ref, act_ref) = refs[:groups], refs[groups:-3], refs[-3:]

    @pl.when(pl.program_id(0) == 0)
    def _():
        x_ref[...] = jnp.concatenate([block[...] for block in blocks], axis=0)

    x = x_ref[...]
    gate_pre = dot_nn(x, gate_ref[0])
    up_pre = dot_nn(x, up_ref[0])
    pre_ref[0] = gate_pre
    pre_ref[1] = up_pre
    act_ref[...] = (gate_pre * jax.nn.sigmoid(gate_pre) * up_pre).astype(BF16)


def backward(c_ref, down_ref, pre_ref, grad_ref):
    hidden_grad = dot_nt(c_ref[...], down_ref[0])
    gate_pre, up_pre = pre_ref[0], pre_ref[1]
    s = jax.nn.sigmoid(gate_pre)
    grad_ref[0] = (hidden_grad * up_pre * s * (1.0 + gate_pre * (1.0 - s))).astype(BF16)
    grad_ref[1] = (hidden_grad * gate_pre * s).astype(BF16)


def join(*refs):
    blocks, out_ref = refs[:-1], refs[-1]
    out_ref[...] = jnp.concatenate([block[...] for block in blocks], axis=0)


def expert_rows(cap, act_ref, down_ref, *outs):
    rows = dot_nn(act_ref[...], down_ref[0])
    for b, out in enumerate(outs):
        out[...] = rows[b * cap : (b + 1) * cap].astype(BF16)


def input_rows(cap, grad_ref, gate_ref, up_ref, *outs):
    rows = dot_nt(grad_ref[0], gate_ref[0]) + dot_nt(grad_ref[1], up_ref[0])
    for b, out in enumerate(outs):
        out[...] = rows[b * cap : (b + 1) * cap].astype(BF16)


def both(own_ref, other_ref, *at):
    if at:
        return jnp.concatenate([own_ref[at[0]], other_ref[at[0]]], axis=0)
    return jnp.concatenate([own_ref[...], other_ref[...]], axis=0)


def store_at_step(outs, value):
    for n, out in enumerate(outs):

        @pl.when(pl.program_id(0) == n)
        def _(out=out):
            out[...] = value


def turn(own_ref, other_ref, out_ref):
    out_ref[...] = both(own_ref, other_ref).T


def turned(name, own, other):
    rows, width = own.shape
    tile = tile_of(width, 256)
    block = pl.BlockSpec((rows, tile), lambda n: (0, n))
    return pl.pallas_call(
        turn,
        out_shape=jax.ShapeDtypeStruct((width, 2 * rows), BF16),
        grid=(width // tile,),
        in_specs=[block] * 2,
        out_specs=pl.BlockSpec((tile, 2 * rows), lambda n: (n, 0)),
        compiler_params=params(),
        cost_estimate=cost(0, 0),
        name=name,
    )(own, other)


def down_share(order_ref, act_ref, c_own, c_other, *outs):
    store_at_step(outs, dot_nn(act_ref[...], both(c_own, c_other)).astype(BF16))


def gate_up_share(count, order_ref, *refs):
    own, other, (g_own, g_other), outs, x_turned = (
        refs[:count],
        refs[count : 2 * count],
        refs[2 * count : 2 * count + 2],
        refs[2 * count + 2 : -1],
        refs[-1],
    )
    cols = own[0].shape[1]

    @pl.when(pl.program_id(0) == 0)
    def _():
        for n in range(count):
            x_turned[n * cols : (n + 1) * cols] = both(own[n], other[n]).T

    for which in range(2):
        share = dot_nn(x_turned[...], both(g_own, g_other, which)).astype(BF16)
        for n in range(count):
            outs[which * count + n][...] = share[n * cols : (n + 1) * cols]


def slot_kernel(*refs):
    parts, (out_ref, wide, sem) = refs[:-3], refs[-3:]
    rows = wide.shape[0] // len(parts)
    for n, part in enumerate(parts):
        wide[n * rows : (n + 1) * rows] = part[...].astype(F32)
    copy = pltpu.make_async_copy(wide, out_ref.at[0], sem)
    copy.start()
    copy.wait()


def slot_of(name, *parts):
    rows, columns = sum(part.shape[0] for part in parts), parts[0].shape[1]
    return pl.pallas_call(
        slot_kernel,
        out_shape=jax.ShapeDtypeStruct((1, rows, columns), F32),
        out_specs=pl.BlockSpec(memory_space=pltpu.HBM),
        scratch_shapes=[pltpu.VMEM((rows, columns), F32), pltpu.SemaphoreType.DMA(())],
        compiler_params=params(),
        cost_estimate=cost(0, 0),
        name=name,
    )(*parts)


def add_kernel(left_ref, right_ref, out_ref):
    out_ref[...] = (left_ref[...].astype(F32) + right_ref[...].astype(F32)).astype(out_ref.dtype)


def added(name, dtype, left, right):
    return pl.pallas_call(
        add_kernel,
        out_shape=jax.ShapeDtypeStruct(left.shape, dtype),
        compiler_params=params(),
        cost_estimate=cost(0, 0),
        name=name,
    )(left, right)


def end_kernel(end_ref, alone_ref, left_ref, right_ref, *outs):
    rows = alone_ref.shape[0] // len(outs)
    for n, out_ref in enumerate(outs):
        at = slice(n * rows, (n + 1) * rows)

        @pl.when(end_ref[0] == 1)
        def _(at=at, out_ref=out_ref):
            out_ref[...] = alone_ref[at]

        @pl.when(end_ref[0] == 0)
        def _(at=at, out_ref=out_ref):
            out_ref[...] = (left_ref[at].astype(F32) + right_ref[at].astype(F32)).astype(BF16)


def at_end(kernel, name, outs, end, *parts):
    smem, vmem = pl.BlockSpec(memory_space=pltpu.SMEM), pl.BlockSpec(memory_space=pltpu.VMEM)
    return pl.pallas_call(
        kernel,
        out_shape=outs,
        in_specs=[smem] + [vmem] * len(parts),
        out_specs=[vmem] * len(outs),
        compiler_params=params(),
        cost_estimate=cost(0, 0),
        name=name,
    )(end, *parts)


def last_share(name, pieces, end, alone, left, right):
    rows, columns = alone.shape
    outs = [jax.ShapeDtypeStruct((rows // pieces, columns), BF16)] * pieces
    return at_end(end_kernel, name, outs, end, alone, left, right)


def final_kernel(at, end_ref, last_ref, near_ref, inner_ref, middle_ref, out_ref):
    last = last_ref[...].astype(F32)

    @pl.when(end_ref[0] == 1)
    def _():
        out_ref[...] = (near_ref[at].astype(F32) + last).astype(BF16)

    @pl.when(end_ref[0] == 0)
    def _():
        inner = inner_ref[at].astype(F32) + middle_ref[...].astype(F32)
        out_ref[...] = (inner + last).astype(BF16)


def final_sum(name, piece, end, last, near, inner, middle):
    at = slice(piece * last.shape[0], (piece + 1) * last.shape[0])
    outs = [jax.ShapeDtypeStruct(last.shape, BF16)]
    return at_end(functools.partial(final_kernel, at), name, outs, end, last, near, inner, middle)[0]


def combine(cap, groups, me_ref, ids_ref, gates_ref, cot_ref, *refs):
    outs, grads = refs[:groups], refs[groups : 2 * groups]
    mixed_ref, token_ref, dots_ref = refs[2 * groups :]
    picks = [pick.astype(BF16) for pick in picks_of(ids_ref[...], cap, groups, me_ref[0])]
    gates = gates_ref[...]
    count, width = mixed_ref.shape
    eye = lax.broadcasted_iota(jnp.int32, (count, count), 0) == lax.broadcasted_iota(
        jnp.int32, (count, count), 1
    )
    weights = [
        jnp.sum(jnp.where(eye, gates[k : k + 1], 0.0), axis=1, keepdims=True)
        for k in range(len(picks))
    ]
    tile = tile_of(width, 512)
    dots = [0.0] * len(picks)
    for start in range(0, width, tile):
        cols = slice(start, start + tile)
        rows = jnp.concatenate([ref[:, cols] for ref in outs], axis=0)
        cot = cot_ref[:, cols].astype(F32)
        mixed = 0.0
        for k, pick in enumerate(picks):
            picked = dot_tn(pick, rows)
            mixed = mixed + weights[k] * picked
            dots[k] = dots[k] + jnp.sum(cot * picked, axis=1, keepdims=True)
        mixed_ref[:, cols] = mixed.astype(BF16)
        rows = jnp.concatenate([ref[:, cols] for ref in grads], axis=0)
        token_ref[:, cols] = dot_tn(sum(picks), rows).astype(BF16)
    dots_ref[...] = jnp.concatenate(
        [jnp.sum(jnp.where(eye, dot, 0.0), axis=0, keepdims=True) for dot in dots], axis=0
    )


def after(value, *others):
    return lax.optimization_barrier((value, others))[0]


def rows_of_core(core, count, cols, own, other):
    rows = jnp.concatenate([own, other], axis=0).reshape(-1, count, 2, cols)
    return lax.dynamic_index_in_dim(rows, core, 2, keepdims=False)


def down_shares(order, cols, act_turned, c_rows, c_other):
    ff, both_rows = act_turned.shape
    total, width = c_rows.shape
    count = order.shape[0]
    block = pl.BlockSpec((total, cols), lambda n, order_ref: (0, order_ref[n]))
    return pl.pallas_call(
        down_share,
        out_shape=[jax.ShapeDtypeStruct((ff, cols), BF16)] * count,
        grid_spec=pltpu.PrefetchScalarGridSpec(
            num_scalar_prefetch=1,
            grid=(count,),
            in_specs=[whole((ff, both_rows))] + [block] * 2,
            out_specs=[whole((ff, cols))] * count,
        ),
        compiler_params=params(),
        cost_estimate=cost(2 * total * width * ff, 5e6),
        name="down_shares",
    )(order, act_turned, c_rows, c_other)


def gate_up_shares(order, cols, x_rows, x_other, grads, grads_other):
    total, width = x_rows.shape
    ff = grads.shape[2]
    count = order.shape[0]
    tile = tile_of(ff, 256)
    columns = [
        pl.BlockSpec((total, cols), lambda j, order_ref, n=n: (0, order_ref[n])) for n in range(count)
    ]
    return pl.pallas_call(
        functools.partial(gate_up_share, count),
        out_shape=[jax.ShapeDtypeStruct((cols, ff), BF16)] * (2 * count),
        grid_spec=pltpu.PrefetchScalarGridSpec(
            num_scalar_prefetch=1,
            grid=(ff // tile,),
            in_specs=columns * 2 + [pl.BlockSpec((2, total, tile), lambda j, _: (0, 0, j))] * 2,
            out_specs=[pl.BlockSpec((cols, tile), lambda j, _: (0, j))] * (2 * count),
            scratch_shapes=[pltpu.VMEM((count * cols, 2 * total), BF16)],
        ),
        compiler_params=params(),
        cost_estimate=cost(4 * total * width * ff, 9e6),
        name="gate_up_shares",
    )(order, *[x_rows] * count, *[x_other] * count, grads, grads_other)


def add(part, own):
    return (part.astype(F32) + own.astype(F32)).astype(BF16)


class LineSum:
    def __init__(self, share, chips, chip):
        self.share, self.chips, self.chip = share, chips, chip
        self.got = None
        self.steps = 0

    def share_at(self, index):
        index = jnp.clip(index, 0, self.chips - 1)
        return lax.dynamic_index_in_dim(self.share, index, 0, keepdims=False)

    def pairs(self, s):
        last = self.chips - 1
        up = [(i, i + 1) for i in range(s)]
        down = [(last - a, last - b) for a, b in up]
        return [[(2 * a + c, 2 * b + c) for a, b in way for c in (0, 1)] for way in (up, down)]

    def message(self, index, side):
        own = self.share_at(index)
        return own if self.got is None else add(self.got[side], own)

    def step(self):
        self.steps += 1
        s, chip, chips = self.steps, self.chip, self.chips
        up, down = self.pairs(s)
        if 2 * s < chips - 1:
            index = jnp.where(chip < s, chips - s + chip, chip - chips + s)
            sent = lax.ppermute(self.message(index, 0), "dp", up + down)
            self.got = (sent, sent)
        else:
            self.got = (
                lax.ppermute(self.message(chips - s + chip, 0), "dp", up),
                lax.ppermute(self.message(chip - chips + s, 1), "dp", down),
            )

    def total(self):
        own = self.share_at(self.chip).astype(F32)
        return (own + self.got[0].astype(F32) + self.got[1].astype(F32)).astype(BF16)


def relocated(total, turn, partner, me, groups):
    if turn is not None:
        return lax.ppermute(total, "expert", [(i, i ^ turn) for i in range(groups)]).astype(F32)[None]
    is_mate = (partner == me)[:, None, None]
    parts = jnp.where(is_mate, total[None], jnp.zeros_like(total)[None])
    parts = lax.all_to_all(parts, "expert", split_axis=0, concat_axis=0, tiled=True)
    mate = lax.dynamic_index_in_dim(partner, me, 0, keepdims=False)
    return lax.dynamic_index_in_dim(parts, mate, 0, keepdims=True).astype(F32)


def shards(tokens, cotangent, expert_ids, gate_weights, partner, w_gate, w_up, w_down):
    args = (tokens, cotangent, expert_ids.T, gate_weights.T, partner, w_gate, w_up, w_down)
    if lax.axis_size("expert") == 4:
        turns = [functools.partial(layer, turn) for turn in (1, 2, 3)]
        return lax.switch(partner[0] - 1, turns, *args)
    return layer(None, *args)


def layer(turn, tokens, cotangent, ids, gates, partner, w_gate, w_up, w_down):
    groups = lax.axis_size("expert")
    replicas = lax.axis_size("dp")
    me = lax.axis_index("expert")
    replica = lax.axis_index("dp")
    chips, chip, core = replicas // 2, replica // 2, replica % 2
    count, width = tokens.shape
    top = ids.shape[0]
    ff = w_gate.shape[2]
    cap = min(count, 5 * count * top // (4 * groups))
    total = groups * cap
    cols = width // replicas
    me_arr = me.astype(jnp.int32).reshape(1)
    smem = pl.BlockSpec(memory_space=pltpu.SMEM)
    vmem = pl.BlockSpec(memory_space=pltpu.VMEM)
    block_shape = jax.ShapeDtypeStruct((cap, width), BF16)

    def exchange(blocks):
        return [blocks[0]] + [
            lax.ppermute(blocks[b], "expert", [(i, i ^ b) for i in range(groups)])
            for b in range(1, groups)
        ]

    def swap(part):
        return lax.ppermute(part, "dp", [(i, i ^ 1) for i in range(replicas)])

    def joined(blocks, name):
        return pl.pallas_call(
            join,
            out_shape=jax.ShapeDtypeStruct((total, blocks[0].shape[1]), BF16),
            in_specs=[vmem] * groups,
            out_specs=vmem,
            compiler_params=params(),
            cost_estimate=cost(0, 4 * total * blocks[0].shape[1]),
            name=name,
        )(*blocks)

    x_blocks = pl.pallas_call(
        functools.partial(place_tokens, cap, groups),
        out_shape=[block_shape] * groups,
        in_specs=[smem, vmem, vmem],
        out_specs=[vmem] * groups,
        compiler_params=params(),
        name="place_tokens",
    )(me_arr, ids, tokens)
    c_blocks = pl.pallas_call(
        functools.partial(place_grads, cap, groups),
        out_shape=[block_shape] * groups,
        in_specs=[smem, vmem, vmem, vmem],
        out_specs=[vmem] * groups,
        compiler_params=params(),
        name="place_grads",
    )(me_arr, ids, gates, cotangent)
    x_blocks = exchange(x_blocks)
    c_blocks = exchange(c_blocks)

    tile = tile_of(ff, 256)
    x_rows, pre, act = pl.pallas_call(
        functools.partial(forward, cap, groups),
        out_shape=[
            jax.ShapeDtypeStruct((total, width), BF16),
            jax.ShapeDtypeStruct((2, total, ff), F32),
            jax.ShapeDtypeStruct((total, ff), BF16),
        ],
        grid=(ff // tile,),
        in_specs=[whole((cap, width))] * groups
        + [pl.BlockSpec((1, width, tile), lambda j: (0, 0, j))] * 2,
        out_specs=[
            whole((total, width)),
            pl.BlockSpec((2, total, tile), lambda j: (0, 0, j)),
            pl.BlockSpec((total, tile), lambda j: (0, j)),
        ],
        compiler_params=params(),
        cost_estimate=cost(4 * total * width * ff, 10e6),
        name="forward",
    )(*x_blocks, w_gate, w_up)
    act_other = swap(act)

    wide = tile_of(width, 512)

    def run_backward(c_rows):
        return pl.pallas_call(
            backward,
            out_shape=jax.ShapeDtypeStruct((2, total, ff), BF16),
            grid=(ff // tile,),
            in_specs=[
                whole((total, width)),
                pl.BlockSpec((1, tile, width), lambda j: (0, j, 0)),
                pl.BlockSpec((2, total, tile), lambda j: (0, 0, j)),
            ],
            out_specs=pl.BlockSpec((2, total, tile), lambda j: (0, 0, j)),
            compiler_params=params(),
            cost_estimate=cost(2 * total * width * ff, 10e6),
            name="backward",
        )(c_rows, w_down, pre)

    def run_expert_rows(act):
        return pl.pallas_call(
            functools.partial(expert_rows, cap),
            out_shape=[block_shape] * groups,
            grid=(width // wide,),
            in_specs=[whole((total, ff)), pl.BlockSpec((1, ff, wide), lambda j: (0, 0, j))],
            out_specs=[pl.BlockSpec((cap, wide), lambda j: (0, j))] * groups,
            compiler_params=params(),
            cost_estimate=cost(2 * total * width * ff, 5e6),
            name="expert_rows",
        )(act, w_down)

    def run_input_rows(grads):
        return pl.pallas_call(
            functools.partial(input_rows, cap),
            out_shape=[block_shape] * groups,
            grid=(width // wide,),
            in_specs=[whole((2, total, ff))] + [pl.BlockSpec((1, wide, ff), lambda j: (0, j, 0))] * 2,
            out_specs=[pl.BlockSpec((cap, wide), lambda j: (0, j))] * groups,
            compiler_params=params(),
            cost_estimate=cost(4 * total * width * ff, 9e6),
            name="input_rows",
        )(grads, w_gate, w_up)

    def run_combine(out_blocks, grad_blocks):
        return pl.pallas_call(
            functools.partial(combine, cap, groups),
            out_shape=[
                jax.ShapeDtypeStruct((count, width), BF16),
                jax.ShapeDtypeStruct((count, width), BF16),
                jax.ShapeDtypeStruct((top, count), F32),
            ],
            in_specs=[smem] + [vmem] * (3 + 2 * groups),
            out_specs=[vmem] * 3,
            compiler_params=params(),
            cost_estimate=cost(6 * total * width * count, 6e6),
            name="combine",
        )(me_arr, ids, gates, cotangent, *out_blocks, *grad_blocks)

    if turn is not None and chips == 4 and cols % 128 == 0:
        low = chip < 2
        end = ((chip == 0) | (chip == 3)).astype(jnp.int32).reshape(1)
        order = (2 * jnp.where(low, 3 - jnp.arange(4), jnp.arange(4)) + core).astype(jnp.int32)

        def swap_ends(part):
            return lax.ppermute(part, "dp", [(i, i ^ 2) for i in range(replicas)])

        def swap_middle(part):
            pairs = [(2, 4), (4, 2), (3, 5), (5, 3), (0, 1), (1, 0), (6, 7), (7, 6)]
            return lax.ppermute(part, "dp", pairs)

        def to_mate(part):
            return lax.ppermute(part, "expert", [(i, i ^ turn) for i in range(groups)])

        x_other = swap(x_rows)
        c_rows = joined(after(c_blocks, act), "join_grads")
        c_other = swap(c_rows)
        act_turned = turned("turn_act", act, after(act_other, c_rows))
        grads = run_backward(after(c_rows, act_turned))
        grads_other = swap(grads)
        d_a, d_b, d_c, d_d = down_shares(order, cols, act_turned, c_rows, after(c_other, grads))
        d_1 = swap_ends(d_a)
        d_2 = swap_ends(after(d_b, d_a))
        out_rows = run_expert_rows(after(act, d_a, grads))
        out_blocks = exchange(after(out_rows, d_a))
        g_a, g_b, g_c, g_d, u_a, u_b, u_c, u_d = gate_up_shares(
            order, cols, after(x_rows, d_a, out_rows[0]), x_other, grads, grads_other
        )
        grad_rows = run_input_rows(after(grads, g_a))

        m = added("down_mid1", BF16, *after((d_1, d_a), grad_rows[0]))
        d_m1, g_1 = swap_middle(m), swap_ends(after(g_a, m))
        m = added("down_mid2", BF16, *after((d_2, d_b), m, *out_blocks))
        d_m2, u_1 = swap_middle(m), swap_ends(after(u_a, m))
        grad_blocks = [grad_rows[0]]
        for n, part in enumerate(grad_rows[1:], 1):
            part = after(part, grad_blocks[-1], m, out_blocks)
            grad_blocks.append(lax.ppermute(part, "expert", [(i, i ^ n) for i in range(groups)]))

        m = added("gate_mid1", BF16, *after((g_1, g_a), m, grad_blocks[1]))
        g_m1 = swap_middle(m)
        (e,) = last_share("down_last", 1, end, *after((d_c, d_m1, d_d), m))
        d_3 = swap_ends(e)
        m = added("up_mid1", BF16, *after((u_1, u_a), e, d_m2, *grad_blocks[1:3]))
        u_m1, g_2 = swap_middle(m), swap_ends(after(g_b, m))

        t = final_sum("down_sum", 0, end, *after((d_3, d_d, d_c, d_m2), m, *grad_blocks[1:]))
        d_t = to_mate(t)
        (e,) = last_share("gate_last", 1, end, *after((g_c, g_m1, g_d), t))
        g_3 = swap_ends(e)
        m = added("gate_mid2", BF16, *after((g_2, g_b), e))
        g_m2 = swap_middle(m)
        half = u_b.shape[0] // 2
        u_b0, u_b1 = after((u_b[:half], u_b[half:]), m)
        u_20, u_21 = swap_ends(u_b0), swap_ends(u_b1)
        e0, e1 = last_share("up_last", 2, end, *after((u_c, u_m1, u_d), m))
        t = final_sum("gate_sum", 0, end, *after((g_3, g_d, g_c, g_m2), e0, d_t))
        g_t, u_30 = to_mate(t), swap_ends(after(e0, g_3))
        m0 = added("up_mid20", BF16, *after((u_20, u_b0), t))
        u_m20 = swap_middle(m0)
        m1 = added("up_mid21", BF16, *after((u_21, u_b1), m0))
        u_m21, u_31 = swap_middle(m1), swap_ends(after(e1, m0))

        slot_down = slot_of("slot_down", *after((d_t,), m1))
        t0 = final_sum("up_sum0", 0, end, *after((u_30, u_d, u_c, u_m20), slot_down, g_t))
        u_t0 = to_mate(t0)
        t1 = final_sum("up_sum1", 1, end, *after((u_31, u_d, u_c, u_m21), t0))
        u_t1 = to_mate(t1)
        mixed_out, token_grad, gate_grad = run_combine(*after((out_blocks, grad_blocks), t1))
        slot_gate = slot_of("slot_gate", *after((g_t,), mixed_out))
        slot_up = slot_of("slot_up", *after((u_t0, u_t1), slot_gate))
    else:
        c_rows = joined(c_blocks, "join_grads")
        grads = run_backward(c_rows)
        out_blocks = exchange(run_expert_rows(act))
        grad_blocks = exchange(run_input_rows(grads))
        acts = jnp.concatenate([act, act_other], axis=0)
        both_grads = jnp.concatenate([grads, swap(grads)], axis=1)
        c_both = rows_of_core(core, chips, cols, c_rows, swap(c_rows))
        x_both = rows_of_core(core, chips, cols, x_rows, swap(x_rows))

        def dot(spec, left, right):
            return jnp.einsum(spec, left, right, preferred_element_type=F32).astype(BF16)

        lines = [
            LineSum(share, chips, chip)
            for share in (
                dot("rf,rzc->zfc", acts, c_both),
                dot("rzc,rf->zcf", x_both, both_grads[0]),
                dot("rzc,rf->zcf", x_both, both_grads[1]),
            )
        ]
        for _ in range(1, chips):
            for line in lines:
                line.step()
        slot_down, slot_gate, slot_up = [
            relocated(line.total(), turn, partner, me, groups) for line in lines
        ]
        mixed_out, token_grad, gate_grad = run_combine(out_blocks, grad_blocks)

    return mixed_out, token_grad, gate_grad.T, slot_gate, slot_up, slot_down


def solution(mesh):
    rows = P(("dp", "expert"), None)
    in_specs = (
        rows,
        rows,
        rows,
        rows,
        P(),
        P("expert", None, None),
        P("expert", None, None),
        P("expert", None, None),
    )
    out_specs = (
        rows,
        rows,
        rows,
        P("expert", "dp", None),
        P("expert", "dp", None),
        P("expert", None, "dp"),
    )
    return jax.shard_map(shards, mesh=mesh, in_specs=in_specs, out_specs=out_specs, check_vma=False)
```

```python
import functools

import jax
import jax.numpy as jnp
from jax import lax
from jax.experimental import pallas as pl
from jax.experimental.pallas import tpu as pltpu
from jax.sharding import PartitionSpec as P

VMEM_BYTES = 47 * 1024 * 1024
F32 = jnp.float32
BF16 = jnp.bfloat16


def dot_nn(a, b):
    return lax.dot_general(a, b, (((1,), (0,)), ((), ())), preferred_element_type=F32)


def dot_nt(a, b):
    return lax.dot_general(a, b, (((1,), (1,)), ((), ())), preferred_element_type=F32)


def dot_tn(a, b):
    return lax.dot_general(a, b, (((0,), (0,)), ((), ())), preferred_element_type=F32)


def tile_of(size, want):
    while size % want:
        want //= 2
    return want


def params(**more):
    return pltpu.CompilerParams(vmem_limit_bytes=VMEM_BYTES, **more)


def whole(shape):
    return pl.BlockSpec(shape, lambda *_: (0,) * len(shape))


def cost(flops, nbytes):
    return pl.CostEstimate(flops=1000, bytes_accessed=1000, transcendentals=0)


def picks_of(ids, cap, groups, me):
    top, count = ids.shape
    block = jnp.bitwise_xor(ids, me)
    lane = lax.broadcasted_iota(jnp.int32, (max(groups, 8), count), 0)
    named = [(block[k : k + 1] == lane).astype(F32) for k in range(top)]
    earlier = lax.broadcasted_iota(jnp.int32, (count, count), 0) < lax.broadcasted_iota(
        jnp.int32, (count, count), 1
    )
    before = dot_nn(sum(named).astype(BF16), earlier.astype(BF16))
    row = lax.broadcasted_iota(jnp.int32, (groups * cap, count), 0)
    picks = []
    for k in range(top):
        pos = jnp.sum(before * named[k], axis=0, keepdims=True).astype(jnp.int32)
        picks.append(block[k : k + 1] * cap + pos == row)
        before = before + named[k]
    return picks


def place_tokens(cap, groups, me_ref, ids_ref, tok_ref, *outs):
    picks = picks_of(ids_ref[...], cap, groups, me_ref[0])
    rows = dot_nn(sum(pick.astype(BF16) for pick in picks), tok_ref[...])
    for b, out in enumerate(outs):
        out[...] = rows[b * cap : (b + 1) * cap].astype(BF16)


def place_grads(cap, groups, me_ref, ids_ref, gates_ref, cot_ref, *outs):
    picks = picks_of(ids_ref[...], cap, groups, me_ref[0])
    gates = gates_ref[...]
    weight = sum(
        jnp.sum(jnp.where(pick, gates[k : k + 1], 0.0), axis=1, keepdims=True)
        for k, pick in enumerate(picks)
    )
    rows = dot_nn(sum(pick.astype(BF16) for pick in picks), cot_ref[...])
    rows = (rows * weight).astype(BF16)
    for b, out in enumerate(outs):
        out[...] = rows[b * cap : (b + 1) * cap]


def forward(cap, groups, *refs):
    blocks, (gate_ref, up_ref), (x_ref, pre_ref, act_ref) = refs[:groups], refs[groups:-3], refs[-3:]

    @pl.when(pl.program_id(0) == 0)
    def _():
        x_ref[...] = jnp.concatenate([block[...] for block in blocks], axis=0)

    x = x_ref[...]
    gate_pre = dot_nn(x, gate_ref[0])
    up_pre = dot_nn(x, up_ref[0])
    pre_ref[0] = gate_pre
    pre_ref[1] = up_pre
    act_ref[...] = (gate_pre * jax.nn.sigmoid(gate_pre) * up_pre).astype(BF16)


def backward(c_ref, down_ref, pre_ref, grad_ref):
    hidden_grad = dot_nt(c_ref[...], down_ref[0])
    gate_pre, up_pre = pre_ref[0], pre_ref[1]
    s = jax.nn.sigmoid(gate_pre)
    grad_ref[0] = (hidden_grad * up_pre * s * (1.0 + gate_pre * (1.0 - s))).astype(BF16)
    grad_ref[1] = (hidden_grad * gate_pre * s).astype(BF16)


def join(*refs):
    blocks, out_ref = refs[:-1], refs[-1]
    out_ref[...] = jnp.concatenate([block[...] for block in blocks], axis=0)


def result_rows(cap, act_ref, grad_ref, down_ref, gate_ref, up_ref, *outs):
    both_rows = (
        dot_nn(act_ref[...], down_ref[0]),
        dot_nt(grad_ref[0], gate_ref[0]) + dot_nt(grad_ref[1], up_ref[0]),
    )
    for n, rows in enumerate(both_rows):
        for b, out in enumerate(outs):
            out[n] = rows[b * cap : (b + 1) * cap].astype(BF16)


def both(own_ref, other_ref, *at):
    if at:
        return jnp.concatenate([own_ref[at[0]], other_ref[at[0]]], axis=0)
    return jnp.concatenate([own_ref[...], other_ref[...]], axis=0)


def store_at_step(outs, value):
    for n, out in enumerate(outs):

        @pl.when(pl.program_id(0) == n)
        def _(out=out):
            out[...] = value


def store_at_step(outs, value):
    for n, out in enumerate(outs):

        @pl.when(pl.program_id(0) == n)
        def _(out=out):
            out[...] = value


def turn(own_ref, other_ref, out_ref):
    out_ref[...] = both(own_ref, other_ref).T


def turned(name, own, other):
    rows, width = own.shape
    tile = tile_of(width, 256)
    block = pl.BlockSpec((rows, tile), lambda n: (0, n))
    return pl.pallas_call(
        turn,
        out_shape=jax.ShapeDtypeStruct((width, 2 * rows), BF16),
        grid=(width // tile,),
        in_specs=[block] * 2,
        out_specs=pl.BlockSpec((tile, 2 * rows), lambda n: (n, 0)),
        compiler_params=params(),
        cost_estimate=cost(0, 0),
        name=name,
    )(own, other)


def down_share(order_ref, act_own, act_other, c_own, c_other, *outs_and_turned):
    *outs, act_turned = outs_and_turned

    @pl.when(pl.program_id(0) == 0)
    def _():
        act_turned[...] = both(act_own, act_other).T

    store_at_step(outs, dot_nn(act_turned[...], both(c_own, c_other)).astype(BF16))


def gate_up_share(count, order_ref, *refs):
    own, other, (g_own, g_other), outs, x_turned = (
        refs[:count],
        refs[count : 2 * count],
        refs[2 * count : 2 * count + 2],
        refs[2 * count + 2 : -1],
        refs[-1],
    )
    cols = own[0].shape[1]

    @pl.when(pl.program_id(0) == 0)
    def _():
        for n in range(count):
            x_turned[n * cols : (n + 1) * cols] = both(own[n], other[n]).T

    for which in range(2):
        share = dot_nn(x_turned[...], both(g_own, g_other, which)).astype(BF16)
        for n in range(count):
            outs[which * count + n][...] = share[n * cols : (n + 1) * cols]


def slot_kernel(*refs):
    parts, (out_ref, wide, sem) = refs[:-3], refs[-3:]
    rows = wide.shape[0] // len(parts)
    for n, part in enumerate(parts):
        wide[n * rows : (n + 1) * rows] = part[...].astype(F32)
    copy = pltpu.make_async_copy(wide, out_ref.at[0], sem)
    copy.start()
    copy.wait()


def slot_of(name, *parts):
    rows, columns = sum(part.shape[0] for part in parts), parts[0].shape[1]
    return pl.pallas_call(
        slot_kernel,
        out_shape=jax.ShapeDtypeStruct((1, rows, columns), F32),
        out_specs=pl.BlockSpec(memory_space=pltpu.HBM),
        scratch_shapes=[pltpu.VMEM((rows, columns), F32), pltpu.SemaphoreType.DMA(())],
        compiler_params=params(),
        cost_estimate=cost(0, 0),
        name=name,
    )(*parts)


def add_kernel(left_ref, right_ref, out_ref):
    out_ref[...] = (left_ref[...].astype(F32) + right_ref[...].astype(F32)).astype(out_ref.dtype)


def added(name, dtype, left, right):
    return pl.pallas_call(
        add_kernel,
        out_shape=jax.ShapeDtypeStruct(left.shape, dtype),
        compiler_params=params(),
        cost_estimate=cost(0, 0),
        name=name,
    )(left, right)


def end_kernel(end_ref, alone_ref, left_ref, right_ref, *outs):
    rows = alone_ref.shape[0] // len(outs)
    for n, out_ref in enumerate(outs):
        at = slice(n * rows, (n + 1) * rows)

        @pl.when(end_ref[0] == 1)
        def _(at=at, out_ref=out_ref):
            out_ref[...] = alone_ref[at]

        @pl.when(end_ref[0] == 0)
        def _(at=at, out_ref=out_ref):
            out_ref[...] = (left_ref[at].astype(F32) + right_ref[at].astype(F32)).astype(BF16)


def at_end(kernel, name, outs, end, *parts):
    smem, vmem = pl.BlockSpec(memory_space=pltpu.SMEM), pl.BlockSpec(memory_space=pltpu.VMEM)
    return pl.pallas_call(
        kernel,
        out_shape=outs,
        in_specs=[smem] + [vmem] * len(parts),
        out_specs=[vmem] * len(outs),
        compiler_params=params(),
        cost_estimate=cost(0, 0),
        name=name,
    )(end, *parts)


def last_share(name, pieces, end, alone, left, right):
    rows, columns = alone.shape
    outs = [jax.ShapeDtypeStruct((rows // pieces, columns), BF16)] * pieces
    return at_end(end_kernel, name, outs, end, alone, left, right)


def final_kernel(at, end_ref, last_ref, near_ref, inner_ref, middle_ref, out_ref):
    last = last_ref[...].astype(F32)

    @pl.when(end_ref[0] == 1)
    def _():
        out_ref[...] = (near_ref[at].astype(F32) + last).astype(BF16)

    @pl.when(end_ref[0] == 0)
    def _():
        inner = inner_ref[at].astype(F32) + middle_ref[...].astype(F32)
        out_ref[...] = (inner + last).astype(BF16)


def final_sum(name, piece, end, last, near, inner, middle):
    at = slice(piece * last.shape[0], (piece + 1) * last.shape[0])
    outs = [jax.ShapeDtypeStruct(last.shape, BF16)]
    return at_end(functools.partial(final_kernel, at), name, outs, end, last, near, inner, middle)[0]


def combine(cap, groups, me_ref, ids_ref, gates_ref, cot_ref, *refs):
    results = refs[:groups]
    mixed_ref, token_ref, dots_ref = refs[groups:]
    picks = [pick.astype(BF16) for pick in picks_of(ids_ref[...], cap, groups, me_ref[0])]
    gates = gates_ref[...]
    count, width = mixed_ref.shape
    eye = lax.broadcasted_iota(jnp.int32, (count, count), 0) == lax.broadcasted_iota(
        jnp.int32, (count, count), 1
    )
    weights = [
        jnp.sum(jnp.where(eye, gates[k : k + 1], 0.0), axis=1, keepdims=True)
        for k in range(len(picks))
    ]
    tile = tile_of(width, 512)
    dots = [0.0] * len(picks)
    for start in range(0, width, tile):
        cols = slice(start, start + tile)
        rows = jnp.concatenate([ref[0, :, cols] for ref in results], axis=0)
        cot = cot_ref[:, cols].astype(F32)
        mixed = 0.0
        for k, pick in enumerate(picks):
            picked = dot_tn(pick, rows)
            mixed = mixed + weights[k] * picked
            dots[k] = dots[k] + jnp.sum(cot * picked, axis=1, keepdims=True)
        mixed_ref[:, cols] = mixed.astype(BF16)
        rows = jnp.concatenate([ref[1, :, cols] for ref in results], axis=0)
        token_ref[:, cols] = dot_tn(sum(picks), rows).astype(BF16)
    dots_ref[...] = jnp.concatenate(
        [jnp.sum(jnp.where(eye, dot, 0.0), axis=0, keepdims=True) for dot in dots], axis=0
    )


def after(value, *others):
    return lax.optimization_barrier((value, others))[0]


def rows_of_core(core, count, cols, own, other):
    rows = jnp.concatenate([own, other], axis=0).reshape(-1, count, 2, cols)
    return lax.dynamic_index_in_dim(rows, core, 2, keepdims=False)


def down_shares(order, cols, act, act_other, c_rows, c_other):
    total, ff = act.shape
    width = c_rows.shape[1]
    count = order.shape[0]
    block = pl.BlockSpec((total, cols), lambda n, order_ref: (0, order_ref[n]))
    return pl.pallas_call(
        down_share,
        out_shape=[jax.ShapeDtypeStruct((ff, cols), BF16)] * count,
        grid_spec=pltpu.PrefetchScalarGridSpec(
            num_scalar_prefetch=1,
            grid=(count,),
            in_specs=[whole((total, ff))] * 2 + [block] * 2,
            out_specs=[whole((ff, cols))] * count,
            scratch_shapes=[pltpu.VMEM((ff, 2 * total), BF16)],
        ),
        compiler_params=params(),
        cost_estimate=cost(2 * total * width * ff, 5e6),
        name="down_shares",
    )(order, act, act_other, c_rows, c_other)


def gate_up_shares(order, cols, x_rows, x_other, grads, grads_other):
    total, width = x_rows.shape
    ff = grads.shape[2]
    count = order.shape[0]
    tile = tile_of(ff, 256)
    columns = [
        pl.BlockSpec((total, cols), lambda j, order_ref, n=n: (0, order_ref[n])) for n in range(count)
    ]
    return pl.pallas_call(
        functools.partial(gate_up_share, count),
        out_shape=[jax.ShapeDtypeStruct((cols, ff), BF16)] * (2 * count),
        grid_spec=pltpu.PrefetchScalarGridSpec(
            num_scalar_prefetch=1,
            grid=(ff // tile,),
            in_specs=columns * 2 + [pl.BlockSpec((2, total, tile), lambda j, _: (0, 0, j))] * 2,
            out_specs=[pl.BlockSpec((cols, tile), lambda j, _: (0, j))] * (2 * count),
            scratch_shapes=[pltpu.VMEM((count * cols, 2 * total), BF16)],
        ),
        compiler_params=params(),
        cost_estimate=cost(4 * total * width * ff, 9e6),
        name="gate_up_shares",
    )(order, *[x_rows] * count, *[x_other] * count, grads, grads_other)


def add(part, own):
    return (part.astype(F32) + own.astype(F32)).astype(BF16)


class LineSum:
    def __init__(self, share, chips, chip):
        self.share, self.chips, self.chip = share, chips, chip
        self.got = None
        self.steps = 0

    def share_at(self, index):
        index = jnp.clip(index, 0, self.chips - 1)
        return lax.dynamic_index_in_dim(self.share, index, 0, keepdims=False)

    def pairs(self, s):
        last = self.chips - 1
        up = [(i, i + 1) for i in range(s)]
        down = [(last - a, last - b) for a, b in up]
        return [[(2 * a + c, 2 * b + c) for a, b in way for c in (0, 1)] for way in (up, down)]

    def message(self, index, side):
        own = self.share_at(index)
        return own if self.got is None else add(self.got[side], own)

    def step(self):
        self.steps += 1
        s, chip, chips = self.steps, self.chip, self.chips
        up, down = self.pairs(s)
        if 2 * s < chips - 1:
            index = jnp.where(chip < s, chips - s + chip, chip - chips + s)
            sent = lax.ppermute(self.message(index, 0), "dp", up + down)
            self.got = (sent, sent)
        else:
            self.got = (
                lax.ppermute(self.message(chips - s + chip, 0), "dp", up),
                lax.ppermute(self.message(chip - chips + s, 1), "dp", down),
            )

    def total(self):
        own = self.share_at(self.chip).astype(F32)
        return (own + self.got[0].astype(F32) + self.got[1].astype(F32)).astype(BF16)


def relocated(total, turn, partner, me, groups):
    if turn is not None:
        return lax.ppermute(total, "expert", [(i, i ^ turn) for i in range(groups)]).astype(F32)[None]
    is_mate = (partner == me)[:, None, None]
    parts = jnp.where(is_mate, total[None], jnp.zeros_like(total)[None])
    parts = lax.all_to_all(parts, "expert", split_axis=0, concat_axis=0, tiled=True)
    mate = lax.dynamic_index_in_dim(partner, me, 0, keepdims=False)
    return lax.dynamic_index_in_dim(parts, mate, 0, keepdims=True).astype(F32)


def shards(tokens, cotangent, expert_ids, gate_weights, partner, w_gate, w_up, w_down):
    args = (tokens, cotangent, expert_ids.T, gate_weights.T, partner, w_gate, w_up, w_down)
    if lax.axis_size("expert") == 4:
        turns = [functools.partial(layer, turn) for turn in (1, 2, 3)]
        return lax.switch(partner[0] - 1, turns, *args)
    return layer(None, *args)


def layer(turn, tokens, cotangent, ids, gates, partner, w_gate, w_up, w_down):
    groups = lax.axis_size("expert")
    replicas = lax.axis_size("dp")
    me = lax.axis_index("expert")
    replica = lax.axis_index("dp")
    chips, chip, core = replicas // 2, replica // 2, replica % 2
    count, width = tokens.shape
    top = ids.shape[0]
    ff = w_gate.shape[2]
    cap = min(count, 5 * count * top // (4 * groups))
    total = groups * cap
    cols = width // replicas
    me_arr = me.astype(jnp.int32).reshape(1)
    smem = pl.BlockSpec(memory_space=pltpu.SMEM)
    vmem = pl.BlockSpec(memory_space=pltpu.VMEM)
    block_shape = jax.ShapeDtypeStruct((cap, width), BF16)

    def exchange(blocks):
        return [blocks[0]] + [
            lax.ppermute(blocks[b], "expert", [(i, i ^ b) for i in range(groups)])
            for b in range(1, groups)
        ]

    def swap(part):
        return lax.ppermute(part, "dp", [(i, i ^ 1) for i in range(replicas)])

    def joined(blocks, name):
        return pl.pallas_call(
            join,
            out_shape=jax.ShapeDtypeStruct((total, blocks[0].shape[1]), BF16),
            in_specs=[vmem] * groups,
            out_specs=vmem,
            compiler_params=params(),
            cost_estimate=cost(0, 4 * total * blocks[0].shape[1]),
            name=name,
        )(*blocks)

    x_blocks = pl.pallas_call(
        functools.partial(place_tokens, cap, groups),
        out_shape=[block_shape] * groups,
        in_specs=[smem, vmem, vmem],
        out_specs=[vmem] * groups,
        compiler_params=params(),
        name="place_tokens",
    )(me_arr, ids, tokens)
    c_blocks = pl.pallas_call(
        functools.partial(place_grads, cap, groups),
        out_shape=[block_shape] * groups,
        in_specs=[smem, vmem, vmem, vmem],
        out_specs=[vmem] * groups,
        compiler_params=params(),
        name="place_grads",
    )(me_arr, ids, gates, cotangent)
    x_blocks = exchange(x_blocks)
    c_blocks = exchange(c_blocks)

    tile = tile_of(ff, 256)
    x_rows, pre, act = pl.pallas_call(
        functools.partial(forward, cap, groups),
        out_shape=[
            jax.ShapeDtypeStruct((total, width), BF16),
            jax.ShapeDtypeStruct((2, total, ff), F32),
            jax.ShapeDtypeStruct((total, ff), BF16),
        ],
        grid=(ff // tile,),
        in_specs=[whole((cap, width))] * groups
        + [pl.BlockSpec((1, width, tile), lambda j: (0, 0, j))] * 2,
        out_specs=[
            whole((total, width)),
            pl.BlockSpec((2, total, tile), lambda j: (0, 0, j)),
            pl.BlockSpec((total, tile), lambda j: (0, j)),
        ],
        compiler_params=params(),
        cost_estimate=cost(4 * total * width * ff, 10e6),
        name="forward",
    )(*x_blocks, w_gate, w_up)
    act_other = swap(act)

    wide = tile_of(width, 512)

    def run_backward(c_rows):
        return pl.pallas_call(
            backward,
            out_shape=jax.ShapeDtypeStruct((2, total, ff), BF16),
            grid=(ff // tile,),
            in_specs=[
                whole((total, width)),
                pl.BlockSpec((1, tile, width), lambda j: (0, j, 0)),
                pl.BlockSpec((2, total, tile), lambda j: (0, 0, j)),
            ],
            out_specs=pl.BlockSpec((2, total, tile), lambda j: (0, 0, j)),
            compiler_params=params(),
            cost_estimate=cost(2 * total * width * ff, 10e6),
            name="backward",
        )(c_rows, w_down, pre)

    def run_result_rows(act, grads):
        return pl.pallas_call(
            functools.partial(result_rows, cap),
            out_shape=[jax.ShapeDtypeStruct((2, cap, width), BF16)] * groups,
            grid=(width // wide,),
            in_specs=[
                whole((total, ff)),
                whole((2, total, ff)),
                pl.BlockSpec((1, ff, wide), lambda j: (0, 0, j)),
                pl.BlockSpec((1, wide, ff), lambda j: (0, j, 0)),
                pl.BlockSpec((1, wide, ff), lambda j: (0, j, 0)),
            ],
            out_specs=[pl.BlockSpec((2, cap, wide), lambda j: (0, 0, j))] * groups,
            compiler_params=params(),
            cost_estimate=cost(6 * total * width * ff, 13e6),
            name="result_rows",
        )(act, grads, w_down, w_gate, w_up)

    def run_combine(results):
        return pl.pallas_call(
            functools.partial(combine, cap, groups),
            out_shape=[
                jax.ShapeDtypeStruct((count, width), BF16),
                jax.ShapeDtypeStruct((count, width), BF16),
                jax.ShapeDtypeStruct((top, count), F32),
            ],
            in_specs=[smem] + [vmem] * (3 + groups),
            out_specs=[vmem] * 3,
            compiler_params=params(),
            cost_estimate=cost(6 * total * width * count, 6e6),
            name="combine",
        )(me_arr, ids, gates, cotangent, *results)

    if turn is not None and chips == 4 and cols % 128 == 0:
        low = chip < 2
        end = ((chip == 0) | (chip == 3)).astype(jnp.int32).reshape(1)
        order = (2 * jnp.where(low, 3 - jnp.arange(4), jnp.arange(4)) + core).astype(jnp.int32)

        def swap_ends(part):
            return lax.ppermute(part, "dp", [(i, i ^ 2) for i in range(replicas)])

        def swap_middle(part):
            pairs = [(2, 4), (4, 2), (3, 5), (5, 3), (0, 1), (1, 0), (6, 7), (7, 6)]
            return lax.ppermute(part, "dp", pairs)

        def to_mate(part):
            return lax.ppermute(part, "expert", [(i, i ^ turn) for i in range(groups)])

        c_rows = joined(after(c_blocks, act), "join_grads")
        c_other = swap(c_rows)
        grads = run_backward(after(c_rows, act_other))
        x_other = swap(after(x_rows, grads))
        grads_other = swap(grads)
        d_a, d_b, d_c, d_d = down_shares(order, cols, act, act_other, c_rows, after(c_other, grads))
        d_1 = swap_ends(d_a)
        d_2 = swap_ends(after(d_b, d_a))
        g_a, g_b, g_c, g_d, u_a, u_b, u_c, u_d = gate_up_shares(
            order, cols, after(x_rows, d_a), x_other, grads, grads_other
        )
        rows = run_result_rows(act, after(grads, g_a))

        m = added("down_mid1", BF16, *after((d_1, d_a), *rows))
        d_m1, g_1 = swap_middle(m), swap_ends(after(g_a, m))
        m = added("down_mid2", BF16, *after((d_2, d_b), m))
        d_m2, u_1 = swap_middle(m), swap_ends(after(u_a, m))
        results = [rows[0]]
        for n, part in enumerate(rows[1:], 1):
            part = after(part, m) if n < groups - 1 else after(part, results[-1], m)
            results.append(lax.ppermute(part, "expert", [(i, i ^ n) for i in range(groups)]))

        m = added("gate_mid1", BF16, *after((g_1, g_a), m))
        g_m1 = swap_middle(m)
        (e,) = last_share("down_last", 1, end, *after((d_c, d_m1, d_d), m))
        d_3 = swap_ends(e)
        m = added("up_mid1", BF16, *after((u_1, u_a), e, d_m2, results[1]))
        u_m1, g_2 = swap_middle(m), swap_ends(after(g_b, m))
        t = final_sum("down_sum", 0, end, *after((d_3, d_d, d_c, d_m2), m))
        d_t = to_mate(t)
        (e,) = last_share("gate_last", 1, end, *after((g_c, g_m1, g_d), t))
        g_3 = swap_ends(e)
        m = added("gate_mid2", BF16, *after((g_2, g_b), e, results[2]))
        g_m2 = swap_middle(m)
        half = u_b.shape[0] // 2
        u_b0, u_b1 = after((u_b[:half], u_b[half:]), m)
        u_20, u_21 = swap_ends(u_b0), swap_ends(u_b1)
        e0, e1 = last_share("up_last", 2, end, *after((u_c, u_m1, u_d), m))
        t = final_sum("gate_sum", 0, end, *after((g_3, g_d, g_c, g_m2), e0, d_t))
        g_t, u_30 = to_mate(t), swap_ends(after(e0, g_3))
        m0 = added("up_mid20", BF16, *after((u_20, u_b0), t))
        u_m20 = swap_middle(m0)
        m1 = added("up_mid21", BF16, *after((u_21, u_b1), m0))
        u_m21, u_31 = swap_middle(m1), swap_ends(after(e1, m0))

        mixed_out, token_grad, gate_grad = run_combine(after(results, m1))
        slot_down = slot_of("slot_down", *after((d_t,), mixed_out))
        t0 = final_sum("up_sum0", 0, end, *after((u_30, u_d, u_c, u_m20), slot_down, g_t))
        u_t0 = to_mate(t0)
        t1 = final_sum("up_sum1", 1, end, *after((u_31, u_d, u_c, u_m21), t0))
        u_t1 = to_mate(t1)
        slot_gate = slot_of("slot_gate", *after((g_t,), t1))
        slot_up = slot_of("slot_up", *after((u_t0, u_t1), slot_gate))
    else:
        c_rows = joined(c_blocks, "join_grads")
        grads = run_backward(c_rows)
        results = exchange(run_result_rows(act, grads))
        acts = jnp.concatenate([act, act_other], axis=0)
        both_grads = jnp.concatenate([grads, swap(grads)], axis=1)
        c_both = rows_of_core(core, chips, cols, c_rows, swap(c_rows))
        x_both = rows_of_core(core, chips, cols, x_rows, swap(x_rows))

        def dot(spec, left, right):
            return jnp.einsum(spec, left, right, preferred_element_type=F32).astype(BF16)

        lines = [
            LineSum(share, chips, chip)
            for share in (
                dot("rf,rzc->zfc", acts, c_both),
                dot("rzc,rf->zcf", x_both, both_grads[0]),
                dot("rzc,rf->zcf", x_both, both_grads[1]),
            )
        ]
        for _ in range(1, chips):
            for line in lines:
                line.step()
        slot_down, slot_gate, slot_up = [
            relocated(line.total(), turn, partner, me, groups) for line in lines
        ]
        mixed_out, token_grad, gate_grad = run_combine(results)

    return mixed_out, token_grad, gate_grad.T, slot_gate, slot_up, slot_down


def solution(mesh):
    rows = P(("dp", "expert"), None)
    in_specs = (
        rows,
        rows,
        rows,
        rows,
        P(),
        P("expert", None, None),
        P("expert", None, None),
        P("expert", None, None),
    )
    out_specs = (
        rows,
        rows,
        rows,
        P("expert", "dp", None),
        P("expert", "dp", None),
        P("expert", None, "dp"),
    )
    return jax.shard_map(shards, mesh=mesh, in_specs=in_specs, out_specs=out_specs, check_vma=False)
```

```python
import functools

import jax
import jax.numpy as jnp
from jax import lax
from jax.experimental import pallas as pl
from jax.experimental.pallas import tpu as pltpu
from jax.sharding import PartitionSpec as P

VMEM_BYTES = 47 * 1024 * 1024
F32 = jnp.float32
BF16 = jnp.bfloat16


def dot_nn(a, b):
    return lax.dot_general(a, b, (((1,), (0,)), ((), ())), preferred_element_type=F32)


def dot_nt(a, b):
    return lax.dot_general(a, b, (((1,), (1,)), ((), ())), preferred_element_type=F32)


def dot_tn(a, b):
    return lax.dot_general(a, b, (((0,), (0,)), ((), ())), preferred_element_type=F32)


def tile_of(size, want):
    while size % want:
        want //= 2
    return want


def params(**more):
    return pltpu.CompilerParams(vmem_limit_bytes=VMEM_BYTES, **more)


def whole(shape):
    return pl.BlockSpec(shape, lambda *_: (0,) * len(shape))


def cost(flops, nbytes):
    return pl.CostEstimate(flops=1000, bytes_accessed=1000, transcendentals=0)


def picks_of(ids, cap, groups, me):
    top, count = ids.shape
    block = jnp.bitwise_xor(ids, me)
    lane = lax.broadcasted_iota(jnp.int32, (max(groups, 8), count), 0)
    named = [(block[k : k + 1] == lane).astype(F32) for k in range(top)]
    earlier = lax.broadcasted_iota(jnp.int32, (count, count), 0) < lax.broadcasted_iota(
        jnp.int32, (count, count), 1
    )
    before = dot_nn(sum(named).astype(BF16), earlier.astype(BF16))
    row = lax.broadcasted_iota(jnp.int32, (groups * cap, count), 0)
    picks = []
    for k in range(top):
        pos = jnp.sum(before * named[k], axis=0, keepdims=True).astype(jnp.int32)
        picks.append(block[k : k + 1] * cap + pos == row)
        before = before + named[k]
    return picks


def place_tokens(cap, groups, me_ref, ids_ref, tok_ref, *outs):
    picks = picks_of(ids_ref[...], cap, groups, me_ref[0])
    rows = dot_nn(sum(pick.astype(BF16) for pick in picks), tok_ref[...])
    for b, out in enumerate(outs):
        out[...] = rows[b * cap : (b + 1) * cap].astype(BF16)


def place_grads(cap, groups, me_ref, ids_ref, gates_ref, cot_ref, *outs):
    picks = picks_of(ids_ref[...], cap, groups, me_ref[0])
    gates = gates_ref[...]
    weight = sum(
        jnp.sum(jnp.where(pick, gates[k : k + 1], 0.0), axis=1, keepdims=True)
        for k, pick in enumerate(picks)
    )
    rows = dot_nn(sum(pick.astype(BF16) for pick in picks), cot_ref[...])
    rows = (rows * weight).astype(BF16)
    for b, out in enumerate(outs):
        out[...] = rows[b * cap : (b + 1) * cap]


def forward(cap, groups, *refs):
    blocks, (gate_ref, up_ref), (x_ref, pre_ref, act_ref) = refs[:groups], refs[groups:-3], refs[-3:]

    @pl.when(pl.program_id(0) == 0)
    def _():
        x_ref[...] = jnp.concatenate([block[...] for block in blocks], axis=0)

    x = x_ref[...]
    gate_pre = dot_nn(x, gate_ref[0])
    up_pre = dot_nn(x, up_ref[0])
    pre_ref[0] = gate_pre
    pre_ref[1] = up_pre
    act_ref[...] = (gate_pre * jax.nn.sigmoid(gate_pre) * up_pre).astype(BF16)


def backward(c_ref, down_ref, pre_ref, grad_ref):
    hidden_grad = dot_nt(c_ref[...], down_ref[0])
    gate_pre, up_pre = pre_ref[0], pre_ref[1]
    s = jax.nn.sigmoid(gate_pre)
    grad_ref[0] = (hidden_grad * up_pre * s * (1.0 + gate_pre * (1.0 - s))).astype(BF16)
    grad_ref[1] = (hidden_grad * gate_pre * s).astype(BF16)


def join(*refs):
    blocks, out_ref = refs[:-1], refs[-1]
    out_ref[...] = jnp.concatenate([block[...] for block in blocks], axis=0)


def result_rows(cap, act_ref, grad_ref, down_ref, gate_ref, up_ref, *outs):
    both_rows = (
        dot_nn(act_ref[...], down_ref[0]),
        dot_nt(grad_ref[0], gate_ref[0]) + dot_nt(grad_ref[1], up_ref[0]),
    )
    for n, rows in enumerate(both_rows):
        for b, out in enumerate(outs):
            out[n] = rows[b * cap : (b + 1) * cap].astype(BF16)


def both(own_ref, other_ref, *at):
    if at:
        return jnp.concatenate([own_ref[at[0]], other_ref[at[0]]], axis=0)
    return jnp.concatenate([own_ref[...], other_ref[...]], axis=0)


def store_at_step(outs, value):
    for n, out in enumerate(outs):

        @pl.when(pl.program_id(0) == n)
        def _(out=out):
            out[...] = value


def store_at_step(outs, value):
    for n, out in enumerate(outs):

        @pl.when(pl.program_id(0) == n)
        def _(out=out):
            out[...] = value


def turn(own_ref, other_ref, out_ref):
    out_ref[...] = both(own_ref, other_ref).T


def turned(name, own, other):
    rows, width = own.shape
    tile = tile_of(width, 256)
    block = pl.BlockSpec((rows, tile), lambda n: (0, n))
    return pl.pallas_call(
        turn,
        out_shape=jax.ShapeDtypeStruct((width, 2 * rows), BF16),
        grid=(width // tile,),
        in_specs=[block] * 2,
        out_specs=pl.BlockSpec((tile, 2 * rows), lambda n: (n, 0)),
        compiler_params=params(),
        cost_estimate=cost(0, 0),
        name=name,
    )(own, other)


def down_share(order_ref, act_own, act_other, c_own, c_other, *outs_and_turned):
    *outs, act_turned = outs_and_turned

    @pl.when(pl.program_id(0) == 0)
    def _():
        act_turned[...] = both(act_own, act_other).T

    store_at_step(outs, dot_nn(act_turned[...], both(c_own, c_other)).astype(BF16))


def gate_up_share(count, order_ref, *refs):
    own, other, (g_own, g_other), outs, x_turned = (
        refs[:count],
        refs[count : 2 * count],
        refs[2 * count : 2 * count + 2],
        refs[2 * count + 2 : -1],
        refs[-1],
    )
    cols = own[0].shape[1]

    @pl.when(pl.program_id(0) == 0)
    def _():
        for n in range(count):
            x_turned[n * cols : (n + 1) * cols] = both(own[n], other[n]).T

    for which in range(2):
        share = dot_nn(x_turned[...], both(g_own, g_other, which)).astype(BF16)
        for n in range(count):
            outs[which * count + n][...] = share[n * cols : (n + 1) * cols]


def slot_kernel(*refs):
    parts, (out_ref, wide, sem) = refs[:-3], refs[-3:]
    rows = wide.shape[0] // len(parts)
    for n, part in enumerate(parts):
        wide[n * rows : (n + 1) * rows] = part[...].astype(F32)
    copy = pltpu.make_async_copy(wide, out_ref.at[0], sem)
    copy.start()
    copy.wait()


def slot_of(name, *parts):
    rows, columns = sum(part.shape[0] for part in parts), parts[0].shape[1]
    return pl.pallas_call(
        slot_kernel,
        out_shape=jax.ShapeDtypeStruct((1, rows, columns), F32),
        out_specs=pl.BlockSpec(memory_space=pltpu.HBM),
        scratch_shapes=[pltpu.VMEM((rows, columns), F32), pltpu.SemaphoreType.DMA(())],
        compiler_params=params(),
        cost_estimate=cost(0, 0),
        name=name,
    )(*parts)


def add_kernel(left_ref, right_ref, out_ref):
    out_ref[...] = (left_ref[...].astype(F32) + right_ref[...].astype(F32)).astype(out_ref.dtype)


def added(name, dtype, left, right):
    return pl.pallas_call(
        add_kernel,
        out_shape=jax.ShapeDtypeStruct(left.shape, dtype),
        compiler_params=params(),
        cost_estimate=cost(0, 0),
        name=name,
    )(left, right)


def end_kernel(end_ref, alone_ref, left_ref, right_ref, *outs):
    rows = alone_ref.shape[0] // len(outs)
    for n, out_ref in enumerate(outs):
        at = slice(n * rows, (n + 1) * rows)

        @pl.when(end_ref[0] == 1)
        def _(at=at, out_ref=out_ref):
            out_ref[...] = alone_ref[at]

        @pl.when(end_ref[0] == 0)
        def _(at=at, out_ref=out_ref):
            out_ref[...] = (left_ref[at].astype(F32) + right_ref[at].astype(F32)).astype(BF16)


def at_end(kernel, name, outs, end, *parts):
    smem, vmem = pl.BlockSpec(memory_space=pltpu.SMEM), pl.BlockSpec(memory_space=pltpu.VMEM)
    return pl.pallas_call(
        kernel,
        out_shape=outs,
        in_specs=[smem] + [vmem] * len(parts),
        out_specs=[vmem] * len(outs),
        compiler_params=params(),
        cost_estimate=cost(0, 0),
        name=name,
    )(end, *parts)


def last_share(name, pieces, end, alone, left, right):
    rows, columns = alone.shape
    outs = [jax.ShapeDtypeStruct((rows // pieces, columns), BF16)] * pieces
    return at_end(end_kernel, name, outs, end, alone, left, right)


def final_kernel(at, end_ref, last_ref, near_ref, inner_ref, middle_ref, out_ref):
    last = last_ref[...].astype(F32)

    @pl.when(end_ref[0] == 1)
    def _():
        out_ref[...] = (near_ref[at].astype(F32) + last).astype(BF16)

    @pl.when(end_ref[0] == 0)
    def _():
        inner = inner_ref[at].astype(F32) + middle_ref[...].astype(F32)
        out_ref[...] = (inner + last).astype(BF16)


def final_sum(name, piece, end, last, near, inner, middle):
    at = slice(piece * last.shape[0], (piece + 1) * last.shape[0])
    outs = [jax.ShapeDtypeStruct(last.shape, BF16)]
    return at_end(functools.partial(final_kernel, at), name, outs, end, last, near, inner, middle)[0]


def combine(cap, groups, me_ref, ids_ref, gates_ref, cot_ref, *refs):
    results = refs[:groups]
    mixed_ref, token_ref, dots_ref = refs[groups:]
    picks = [pick.astype(BF16) for pick in picks_of(ids_ref[...], cap, groups, me_ref[0])]
    gates = gates_ref[...]
    count, width = mixed_ref.shape
    eye = lax.broadcasted_iota(jnp.int32, (count, count), 0) == lax.broadcasted_iota(
        jnp.int32, (count, count), 1
    )
    weights = [
        jnp.sum(jnp.where(eye, gates[k : k + 1], 0.0), axis=1, keepdims=True)
        for k in range(len(picks))
    ]
    tile = tile_of(width, 512)
    dots = [0.0] * len(picks)
    for start in range(0, width, tile):
        cols = slice(start, start + tile)
        rows = jnp.concatenate([ref[0, :, cols] for ref in results], axis=0)
        cot = cot_ref[:, cols].astype(F32)
        mixed = 0.0
        for k, pick in enumerate(picks):
            picked = dot_tn(pick, rows)
            mixed = mixed + weights[k] * picked
            dots[k] = dots[k] + jnp.sum(cot * picked, axis=1, keepdims=True)
        mixed_ref[:, cols] = mixed.astype(BF16)
        rows = jnp.concatenate([ref[1, :, cols] for ref in results], axis=0)
        token_ref[:, cols] = dot_tn(sum(picks), rows).astype(BF16)
    dots_ref[...] = jnp.concatenate(
        [jnp.sum(jnp.where(eye, dot, 0.0), axis=0, keepdims=True) for dot in dots], axis=0
    )


def after(value, *others):
    return lax.optimization_barrier((value, others))[0]


def rows_of_core(core, count, cols, own, other):
    rows = jnp.concatenate([own, other], axis=0).reshape(-1, count, 2, cols)
    return lax.dynamic_index_in_dim(rows, core, 2, keepdims=False)


def down_shares(order, cols, act, act_other, c_rows, c_other):
    total, ff = act.shape
    width = c_rows.shape[1]
    count = order.shape[0]
    block = pl.BlockSpec((total, cols), lambda n, order_ref: (0, order_ref[n]))
    return pl.pallas_call(
        down_share,
        out_shape=[jax.ShapeDtypeStruct((ff, cols), BF16)] * count,
        grid_spec=pltpu.PrefetchScalarGridSpec(
            num_scalar_prefetch=1,
            grid=(count,),
            in_specs=[whole((total, ff))] * 2 + [block] * 2,
            out_specs=[whole((ff, cols))] * count,
            scratch_shapes=[pltpu.VMEM((ff, 2 * total), BF16)],
        ),
        compiler_params=params(),
        cost_estimate=cost(2 * total * width * ff, 5e6),
        name="down_shares",
    )(order, act, act_other, c_rows, c_other)


def gate_up_shares(order, cols, x_rows, x_other, grads, grads_other):
    total, width = x_rows.shape
    ff = grads.shape[2]
    count = order.shape[0]
    tile = tile_of(ff, 256)
    columns = [
        pl.BlockSpec((total, cols), lambda j, order_ref, n=n: (0, order_ref[n])) for n in range(count)
    ]
    return pl.pallas_call(
        functools.partial(gate_up_share, count),
        out_shape=[jax.ShapeDtypeStruct((cols, ff), BF16)] * (2 * count),
        grid_spec=pltpu.PrefetchScalarGridSpec(
            num_scalar_prefetch=1,
            grid=(ff // tile,),
            in_specs=columns * 2 + [pl.BlockSpec((2, total, tile), lambda j, _: (0, 0, j))] * 2,
            out_specs=[pl.BlockSpec((cols, tile), lambda j, _: (0, j))] * (2 * count),
            scratch_shapes=[pltpu.VMEM((count * cols, 2 * total), BF16)],
        ),
        compiler_params=params(),
        cost_estimate=cost(4 * total * width * ff, 9e6),
        name="gate_up_shares",
    )(order, *[x_rows] * count, *[x_other] * count, grads, grads_other)


def add(part, own):
    return (part.astype(F32) + own.astype(F32)).astype(BF16)


class LineSum:
    def __init__(self, share, chips, chip):
        self.share, self.chips, self.chip = share, chips, chip
        self.got = None
        self.steps = 0

    def share_at(self, index):
        index = jnp.clip(index, 0, self.chips - 1)
        return lax.dynamic_index_in_dim(self.share, index, 0, keepdims=False)

    def pairs(self, s):
        last = self.chips - 1
        up = [(i, i + 1) for i in range(s)]
        down = [(last - a, last - b) for a, b in up]
        return [[(2 * a + c, 2 * b + c) for a, b in way for c in (0, 1)] for way in (up, down)]

    def message(self, index, side):
        own = self.share_at(index)
        return own if self.got is None else add(self.got[side], own)

    def step(self):
        self.steps += 1
        s, chip, chips = self.steps, self.chip, self.chips
        up, down = self.pairs(s)
        if 2 * s < chips - 1:
            index = jnp.where(chip < s, chips - s + chip, chip - chips + s)
            sent = lax.ppermute(self.message(index, 0), "dp", up + down)
            self.got = (sent, sent)
        else:
            self.got = (
                lax.ppermute(self.message(chips - s + chip, 0), "dp", up),
                lax.ppermute(self.message(chip - chips + s, 1), "dp", down),
            )

    def total(self):
        own = self.share_at(self.chip).astype(F32)
        return (own + self.got[0].astype(F32) + self.got[1].astype(F32)).astype(BF16)


def relocated(total, turn, partner, me, groups):
    if turn is not None:
        return lax.ppermute(total, "expert", [(i, i ^ turn) for i in range(groups)]).astype(F32)[None]
    is_mate = (partner == me)[:, None, None]
    parts = jnp.where(is_mate, total[None], jnp.zeros_like(total)[None])
    parts = lax.all_to_all(parts, "expert", split_axis=0, concat_axis=0, tiled=True)
    mate = lax.dynamic_index_in_dim(partner, me, 0, keepdims=False)
    return lax.dynamic_index_in_dim(parts, mate, 0, keepdims=True).astype(F32)


def shards(tokens, cotangent, expert_ids, gate_weights, partner, w_gate, w_up, w_down):
    args = (tokens, cotangent, expert_ids.T, gate_weights.T, partner, w_gate, w_up, w_down)
    if lax.axis_size("expert") == 4:
        turns = [functools.partial(layer, turn) for turn in (1, 2, 3)]
        return lax.switch(partner[0] - 1, turns, *args)
    return layer(None, *args)


def layer(turn, tokens, cotangent, ids, gates, partner, w_gate, w_up, w_down):
    groups = lax.axis_size("expert")
    replicas = lax.axis_size("dp")
    me = lax.axis_index("expert")
    replica = lax.axis_index("dp")
    chips, chip, core = replicas // 2, replica // 2, replica % 2
    count, width = tokens.shape
    top = ids.shape[0]
    ff = w_gate.shape[2]
    cap = min(count, 5 * count * top // (4 * groups))
    total = groups * cap
    cols = width // replicas
    me_arr = me.astype(jnp.int32).reshape(1)
    smem = pl.BlockSpec(memory_space=pltpu.SMEM)
    vmem = pl.BlockSpec(memory_space=pltpu.VMEM)
    block_shape = jax.ShapeDtypeStruct((cap, width), BF16)

    def exchange(blocks):
        return [blocks[0]] + [
            lax.ppermute(blocks[b], "expert", [(i, i ^ b) for i in range(groups)])
            for b in range(1, groups)
        ]

    def swap(part):
        return lax.ppermute(part, "dp", [(i, i ^ 1) for i in range(replicas)])

    def joined(blocks, name):
        return pl.pallas_call(
            join,
            out_shape=jax.ShapeDtypeStruct((total, blocks[0].shape[1]), BF16),
            in_specs=[vmem] * groups,
            out_specs=vmem,
            compiler_params=params(),
            cost_estimate=cost(0, 4 * total * blocks[0].shape[1]),
            name=name,
        )(*blocks)

    x_blocks = pl.pallas_call(
        functools.partial(place_tokens, cap, groups),
        out_shape=[block_shape] * groups,
        in_specs=[smem, vmem, vmem],
        out_specs=[vmem] * groups,
        compiler_params=params(),
        name="place_tokens",
    )(me_arr, ids, tokens)
    c_blocks = pl.pallas_call(
        functools.partial(place_grads, cap, groups),
        out_shape=[block_shape] * groups,
        in_specs=[smem, vmem, vmem, vmem],
        out_specs=[vmem] * groups,
        compiler_params=params(),
        name="place_grads",
    )(me_arr, ids, gates, cotangent)
    x_blocks = exchange(x_blocks)
    c_blocks = exchange(c_blocks)

    tile = tile_of(ff, 256)
    x_rows, pre, act = pl.pallas_call(
        functools.partial(forward, cap, groups),
        out_shape=[
            jax.ShapeDtypeStruct((total, width), BF16),
            jax.ShapeDtypeStruct((2, total, ff), F32),
            jax.ShapeDtypeStruct((total, ff), BF16),
        ],
        grid=(ff // tile,),
        in_specs=[whole((cap, width))] * groups
        + [pl.BlockSpec((1, width, tile), lambda j: (0, 0, j))] * 2,
        out_specs=[
            whole((total, width)),
            pl.BlockSpec((2, total, tile), lambda j: (0, 0, j)),
            pl.BlockSpec((total, tile), lambda j: (0, j)),
        ],
        compiler_params=params(),
        cost_estimate=cost(4 * total * width * ff, 10e6),
        name="forward",
    )(*x_blocks, w_gate, w_up)
    act_other = swap(act)

    wide = tile_of(width, 1024)

    def run_backward(c_rows):
        return pl.pallas_call(
            backward,
            out_shape=jax.ShapeDtypeStruct((2, total, ff), BF16),
            grid=(ff // tile,),
            in_specs=[
                whole((total, width)),
                pl.BlockSpec((1, tile, width), lambda j: (0, j, 0)),
                pl.BlockSpec((2, total, tile), lambda j: (0, 0, j)),
            ],
            out_specs=pl.BlockSpec((2, total, tile), lambda j: (0, 0, j)),
            compiler_params=params(),
            cost_estimate=cost(2 * total * width * ff, 10e6),
            name="backward",
        )(c_rows, w_down, pre)

    def run_result_rows(act, grads):
        return pl.pallas_call(
            functools.partial(result_rows, cap),
            out_shape=[jax.ShapeDtypeStruct((2, cap, width), BF16)] * groups,
            grid=(width // wide,),
            in_specs=[
                whole((total, ff)),
                whole((2, total, ff)),
                pl.BlockSpec((1, ff, wide), lambda j: (0, 0, j)),
                pl.BlockSpec((1, wide, ff), lambda j: (0, j, 0)),
                pl.BlockSpec((1, wide, ff), lambda j: (0, j, 0)),
            ],
            out_specs=[pl.BlockSpec((2, cap, wide), lambda j: (0, 0, j))] * groups,
            compiler_params=params(),
            cost_estimate=cost(6 * total * width * ff, 13e6),
            name="result_rows",
        )(act, grads, w_down, w_gate, w_up)

    def run_combine(results):
        return pl.pallas_call(
            functools.partial(combine, cap, groups),
            out_shape=[
                jax.ShapeDtypeStruct((count, width), BF16),
                jax.ShapeDtypeStruct((count, width), BF16),
                jax.ShapeDtypeStruct((top, count), F32),
            ],
            in_specs=[smem] + [vmem] * (3 + groups),
            out_specs=[vmem] * 3,
            compiler_params=params(),
            cost_estimate=cost(6 * total * width * count, 6e6),
            name="combine",
        )(me_arr, ids, gates, cotangent, *results)

    if turn is not None and chips == 4 and cols % 128 == 0:
        low = chip < 2
        end = ((chip == 0) | (chip == 3)).astype(jnp.int32).reshape(1)
        order = (2 * jnp.where(low, 3 - jnp.arange(4), jnp.arange(4)) + core).astype(jnp.int32)

        def swap_ends(part):
            return lax.ppermute(part, "dp", [(i, i ^ 2) for i in range(replicas)])

        def swap_middle(part):
            pairs = [(2, 4), (4, 2), (3, 5), (5, 3), (0, 1), (1, 0), (6, 7), (7, 6)]
            return lax.ppermute(part, "dp", pairs)

        def to_mate(part):
            return lax.ppermute(part, "expert", [(i, i ^ turn) for i in range(groups)])

        c_rows = joined(after(c_blocks, act), "join_grads")
        c_other = swap(c_rows)
        grads = run_backward(after(c_rows, act_other))
        x_other = swap(after(x_rows, grads))
        grads_other = swap(grads)
        d_a, d_b, d_c, d_d = down_shares(order, cols, act, act_other, c_rows, after(c_other, grads))
        d_1 = swap_ends(d_a)
        d_2 = swap_ends(after(d_b, d_a))
        g_a, g_b, g_c, g_d, u_a, u_b, u_c, u_d = gate_up_shares(
            order, cols, after(x_rows, d_a), x_other, grads, grads_other
        )
        rows = run_result_rows(act, after(grads, g_a))

        m = added("down_mid1", BF16, *after((d_1, d_a), *rows))
        d_m1, g_1 = swap_middle(m), swap_ends(after(g_a, m))
        m = added("down_mid2", BF16, *after((d_2, d_b), m))
        d_m2, u_1 = swap_middle(m), swap_ends(after(u_a, m))
        results = [rows[0]]
        for n, part in enumerate(rows[1:], 1):
            part = after(part, m) if n < groups - 1 else after(part, results[-1], m)
            results.append(lax.ppermute(part, "expert", [(i, i ^ n) for i in range(groups)]))

        m = added("gate_mid1", BF16, *after((g_1, g_a), m))
        g_m1 = swap_middle(m)
        (e,) = last_share("down_last", 1, end, *after((d_c, d_m1, d_d), m))
        d_3 = swap_ends(e)
        m = added("up_mid1", BF16, *after((u_1, u_a), e, d_m2))
        u_m1, g_2 = swap_middle(m), swap_ends(after(g_b, m))
        t = final_sum("down_sum", 0, end, *after((d_3, d_d, d_c, d_m2), m, results[1]))
        d_t = to_mate(t)
        (e,) = last_share("gate_last", 1, end, *after((g_c, g_m1, g_d), t))
        g_3 = swap_ends(e)
        m = added("gate_mid2", BF16, *after((g_2, g_b), e, results[2]))
        g_m2 = swap_middle(m)
        half = u_b.shape[0] // 2
        u_b0, u_b1 = after((u_b[:half], u_b[half:]), m)
        u_20, u_21 = swap_ends(u_b0), swap_ends(u_b1)
        e0, e1 = last_share("up_last", 2, end, *after((u_c, u_m1, u_d), m))
        t = final_sum("gate_sum", 0, end, *after((g_3, g_d, g_c, g_m2), e0, d_t))
        g_t, u_30 = to_mate(t), swap_ends(after(e0, g_3))
        m0 = added("up_mid20", BF16, *after((u_20, u_b0), t))
        u_m20 = swap_middle(m0)
        m1 = added("up_mid21", BF16, *after((u_21, u_b1), m0))
        u_m21, u_31 = swap_middle(m1), swap_ends(after(e1, m0))

        mixed_out, token_grad, gate_grad = run_combine(after(results, m1))
        slot_down = slot_of("slot_down", *after((d_t,), mixed_out))
        t0 = final_sum("up_sum0", 0, end, *after((u_30, u_d, u_c, u_m20), slot_down, g_t))
        u_t0 = to_mate(t0)
        t1 = final_sum("up_sum1", 1, end, *after((u_31, u_d, u_c, u_m21), t0))
        u_t1 = to_mate(t1)
        slot_gate = slot_of("slot_gate", *after((g_t,), t1))
        slot_up = slot_of("slot_up", *after((u_t0, u_t1), slot_gate))
    else:
        c_rows = joined(c_blocks, "join_grads")
        grads = run_backward(c_rows)
        results = exchange(run_result_rows(act, grads))
        acts = jnp.concatenate([act, act_other], axis=0)
        both_grads = jnp.concatenate([grads, swap(grads)], axis=1)
        c_both = rows_of_core(core, chips, cols, c_rows, swap(c_rows))
        x_both = rows_of_core(core, chips, cols, x_rows, swap(x_rows))

        def dot(spec, left, right):
            return jnp.einsum(spec, left, right, preferred_element_type=F32).astype(BF16)

        lines = [
            LineSum(share, chips, chip)
            for share in (
                dot("rf,rzc->zfc", acts, c_both),
                dot("rzc,rf->zcf", x_both, both_grads[0]),
                dot("rzc,rf->zcf", x_both, both_grads[1]),
            )
        ]
        for _ in range(1, chips):
            for line in lines:
                line.step()
        slot_down, slot_gate, slot_up = [
            relocated(line.total(), turn, partner, me, groups) for line in lines
        ]
        mixed_out, token_grad, gate_grad = run_combine(results)

    return mixed_out, token_grad, gate_grad.T, slot_gate, slot_up, slot_down


def solution(mesh):
    rows = P(("dp", "expert"), None)
    in_specs = (
        rows,
        rows,
        rows,
        rows,
        P(),
        P("expert", None, None),
        P("expert", None, None),
        P("expert", None, None),
    )
    out_specs = (
        rows,
        rows,
        rows,
        P("expert", "dp", None),
        P("expert", "dp", None),
        P("expert", None, "dp"),
    )
    return jax.shard_map(shards, mesh=mesh, in_specs=in_specs, out_specs=out_specs, check_vma=False)
```

```python
import functools

import jax
import jax.numpy as jnp
from jax import lax
from jax.experimental import pallas as pl
from jax.experimental.pallas import tpu as pltpu
from jax.sharding import PartitionSpec as P

VMEM_BYTES = 47 * 1024 * 1024
F32 = jnp.float32
BF16 = jnp.bfloat16


def dot_nn(a, b):
    return lax.dot_general(a, b, (((1,), (0,)), ((), ())), preferred_element_type=F32)


def dot_nt(a, b):
    return lax.dot_general(a, b, (((1,), (1,)), ((), ())), preferred_element_type=F32)


def dot_tn(a, b):
    return lax.dot_general(a, b, (((0,), (0,)), ((), ())), preferred_element_type=F32)


def tile_of(size, want):
    while size % want:
        want //= 2
    return want


def params(**more):
    return pltpu.CompilerParams(vmem_limit_bytes=VMEM_BYTES, **more)


def whole(shape):
    return pl.BlockSpec(shape, lambda *_: (0,) * len(shape))


def cost(flops, nbytes):
    return pl.CostEstimate(flops=1000, bytes_accessed=1000, transcendentals=0)


def picks_of(ids, cap, groups, me):
    top, count = ids.shape
    block = jnp.bitwise_xor(ids, me)
    lane = lax.broadcasted_iota(jnp.int32, (max(groups, 8), count), 0)
    named = [(block[k : k + 1] == lane).astype(F32) for k in range(top)]
    earlier = lax.broadcasted_iota(jnp.int32, (count, count), 0) < lax.broadcasted_iota(
        jnp.int32, (count, count), 1
    )
    before = dot_nn(sum(named).astype(BF16), earlier.astype(BF16))
    row = lax.broadcasted_iota(jnp.int32, (groups * cap, count), 0)
    picks = []
    for k in range(top):
        pos = jnp.sum(before * named[k], axis=0, keepdims=True).astype(jnp.int32)
        picks.append(block[k : k + 1] * cap + pos == row)
        before = before + named[k]
    return picks


def place_tokens(cap, groups, me_ref, ids_ref, tok_ref, *outs):
    picks = picks_of(ids_ref[...], cap, groups, me_ref[0])
    rows = dot_nn(sum(pick.astype(BF16) for pick in picks), tok_ref[...])
    for b, out in enumerate(outs):
        out[...] = rows[b * cap : (b + 1) * cap].astype(BF16)


def place_grads(cap, groups, me_ref, ids_ref, gates_ref, cot_ref, *outs):
    picks = picks_of(ids_ref[...], cap, groups, me_ref[0])
    gates = gates_ref[...]
    weight = sum(
        jnp.sum(jnp.where(pick, gates[k : k + 1], 0.0), axis=1, keepdims=True)
        for k, pick in enumerate(picks)
    )
    rows = dot_nn(sum(pick.astype(BF16) for pick in picks), cot_ref[...])
    rows = (rows * weight).astype(BF16)
    for b, out in enumerate(outs):
        out[...] = rows[b * cap : (b + 1) * cap]


def forward(cap, groups, *refs):
    blocks, (gate_ref, up_ref), (x_ref, pre_ref, act_ref) = refs[:groups], refs[groups:-3], refs[-3:]

    @pl.when(pl.program_id(0) == 0)
    def _():
        x_ref[...] = jnp.concatenate([block[...] for block in blocks], axis=0)

    x = x_ref[...]
    gate_pre = dot_nn(x, gate_ref[0])
    up_pre = dot_nn(x, up_ref[0])
    pre_ref[0] = gate_pre
    pre_ref[1] = up_pre
    act_ref[...] = (gate_pre * jax.nn.sigmoid(gate_pre) * up_pre).astype(BF16)


def backward(c_ref, down_ref, pre_ref, grad_ref):
    hidden_grad = dot_nt(c_ref[...], down_ref[0])
    gate_pre, up_pre = pre_ref[0], pre_ref[1]
    s = jax.nn.sigmoid(gate_pre)
    grad_ref[0] = (hidden_grad * up_pre * s * (1.0 + gate_pre * (1.0 - s))).astype(BF16)
    grad_ref[1] = (hidden_grad * gate_pre * s).astype(BF16)


def join(*refs):
    blocks, out_ref = refs[:-1], refs[-1]
    out_ref[...] = jnp.concatenate([block[...] for block in blocks], axis=0)


def result_rows(cap, act_ref, grad_ref, down_ref, gate_ref, up_ref, *outs):
    both_rows = (
        dot_nn(act_ref[...], down_ref[0]),
        dot_nt(grad_ref[0], gate_ref[0]) + dot_nt(grad_ref[1], up_ref[0]),
    )
    for n, rows in enumerate(both_rows):
        for b, out in enumerate(outs):
            out[n] = rows[b * cap : (b + 1) * cap].astype(BF16)


def both(own_ref, other_ref, *at):
    if at:
        return jnp.concatenate([own_ref[at[0]], other_ref[at[0]]], axis=0)
    return jnp.concatenate([own_ref[...], other_ref[...]], axis=0)


def store_at_step(outs, value):
    for n, out in enumerate(outs):

        @pl.when(pl.program_id(0) == n)
        def _(out=out):
            out[...] = value


def store_at_step(outs, value):
    for n, out in enumerate(outs):

        @pl.when(pl.program_id(0) == n)
        def _(out=out):
            out[...] = value


def turn(own_ref, other_ref, out_ref):
    out_ref[...] = both(own_ref, other_ref).T


def turned(name, own, other):
    rows, width = own.shape
    tile = tile_of(width, 256)
    block = pl.BlockSpec((rows, tile), lambda n: (0, n))
    return pl.pallas_call(
        turn,
        out_shape=jax.ShapeDtypeStruct((width, 2 * rows), BF16),
        grid=(width // tile,),
        in_specs=[block] * 2,
        out_specs=pl.BlockSpec((tile, 2 * rows), lambda n: (n, 0)),
        compiler_params=params(),
        cost_estimate=cost(0, 0),
        name=name,
    )(own, other)


def down_share(order_ref, act_own, act_other, c_own, c_other, *outs_and_turned):
    *outs, act_turned = outs_and_turned

    @pl.when(pl.program_id(0) == 0)
    def _():
        act_turned[...] = both(act_own, act_other).T

    store_at_step(outs, dot_nn(act_turned[...], both(c_own, c_other)).astype(BF16))


def gate_up_share(count, order_ref, *refs):
    own, other, (g_own, g_other), outs, x_turned = (
        refs[:count],
        refs[count : 2 * count],
        refs[2 * count : 2 * count + 2],
        refs[2 * count + 2 : -1],
        refs[-1],
    )
    cols = own[0].shape[1]

    @pl.when(pl.program_id(0) == 0)
    def _():
        for n in range(count):
            x_turned[n * cols : (n + 1) * cols] = both(own[n], other[n]).T

    for which in range(2):
        share = dot_nn(x_turned[...], both(g_own, g_other, which)).astype(BF16)
        for n in range(count):
            outs[which * count + n][...] = share[n * cols : (n + 1) * cols]


def slot_kernel(*refs):
    parts, (out_ref, wide, sem) = refs[:-3], refs[-3:]
    rows = wide.shape[0] // len(parts)
    for n, part in enumerate(parts):
        wide[n * rows : (n + 1) * rows] = part[...].astype(F32)
    copy = pltpu.make_async_copy(wide, out_ref.at[0], sem)
    copy.start()
    copy.wait()


def slot_of(name, *parts):
    rows, columns = sum(part.shape[0] for part in parts), parts[0].shape[1]
    return pl.pallas_call(
        slot_kernel,
        out_shape=jax.ShapeDtypeStruct((1, rows, columns), F32),
        out_specs=pl.BlockSpec(memory_space=pltpu.HBM),
        scratch_shapes=[pltpu.VMEM((rows, columns), F32), pltpu.SemaphoreType.DMA(())],
        compiler_params=params(),
        cost_estimate=cost(0, 0),
        name=name,
    )(*parts)


def add_kernel(left_ref, right_ref, out_ref):
    out_ref[...] = (left_ref[...].astype(F32) + right_ref[...].astype(F32)).astype(out_ref.dtype)


def added(name, dtype, left, right):
    return pl.pallas_call(
        add_kernel,
        out_shape=jax.ShapeDtypeStruct(left.shape, dtype),
        compiler_params=params(),
        cost_estimate=cost(0, 0),
        name=name,
    )(left, right)


def end_kernel(end_ref, alone_ref, left_ref, right_ref, *outs):
    rows = alone_ref.shape[0] // len(outs)
    for n, out_ref in enumerate(outs):
        at = slice(n * rows, (n + 1) * rows)

        @pl.when(end_ref[0] == 1)
        def _(at=at, out_ref=out_ref):
            out_ref[...] = alone_ref[at]

        @pl.when(end_ref[0] == 0)
        def _(at=at, out_ref=out_ref):
            out_ref[...] = (left_ref[at].astype(F32) + right_ref[at].astype(F32)).astype(BF16)


def at_end(kernel, name, outs, end, *parts):
    smem, vmem = pl.BlockSpec(memory_space=pltpu.SMEM), pl.BlockSpec(memory_space=pltpu.VMEM)
    return pl.pallas_call(
        kernel,
        out_shape=outs,
        in_specs=[smem] + [vmem] * len(parts),
        out_specs=[vmem] * len(outs),
        compiler_params=params(),
        cost_estimate=cost(0, 0),
        name=name,
    )(end, *parts)


def last_share(name, pieces, end, alone, left, right):
    rows, columns = alone.shape
    outs = [jax.ShapeDtypeStruct((rows // pieces, columns), BF16)] * pieces
    return at_end(end_kernel, name, outs, end, alone, left, right)


def final_kernel(at, end_ref, last_ref, near_ref, inner_ref, middle_ref, out_ref):
    last = last_ref[...].astype(F32)

    @pl.when(end_ref[0] == 1)
    def _():
        out_ref[...] = (near_ref[at].astype(F32) + last).astype(BF16)

    @pl.when(end_ref[0] == 0)
    def _():
        inner = inner_ref[at].astype(F32) + middle_ref[...].astype(F32)
        out_ref[...] = (inner + last).astype(BF16)


def final_sum(name, piece, end, last, near, inner, middle):
    at = slice(piece * last.shape[0], (piece + 1) * last.shape[0])
    outs = [jax.ShapeDtypeStruct(last.shape, BF16)]
    return at_end(functools.partial(final_kernel, at), name, outs, end, last, near, inner, middle)[0]


def combine(cap, groups, me_ref, ids_ref, gates_ref, cot_ref, *refs):
    results = refs[:groups]
    mixed_ref, token_ref, dots_ref = refs[groups:]
    picks = [pick.astype(BF16) for pick in picks_of(ids_ref[...], cap, groups, me_ref[0])]
    gates = gates_ref[...]
    count, width = mixed_ref.shape
    eye = lax.broadcasted_iota(jnp.int32, (count, count), 0) == lax.broadcasted_iota(
        jnp.int32, (count, count), 1
    )
    weights = [
        jnp.sum(jnp.where(eye, gates[k : k + 1], 0.0), axis=1, keepdims=True)
        for k in range(len(picks))
    ]
    tile = tile_of(width, 512)
    dots = [0.0] * len(picks)
    turned_picks = jnp.concatenate([pick.astype(F32).T for pick in picks], axis=0).astype(BF16)
    turned_sum = sum(pick.astype(F32) for pick in picks).T.astype(BF16)
    for start in range(0, width, tile):
        cols = slice(start, start + tile)
        rows = jnp.concatenate([ref[0, :, cols] for ref in results], axis=0)
        cot = cot_ref[:, cols].astype(F32)
        mixed = 0.0
        both_ranks = dot_nn(turned_picks, rows)
        for k in range(len(picks)):
            picked = both_ranks[k * count : (k + 1) * count]
            mixed = mixed + weights[k] * picked
            dots[k] = dots[k] + jnp.sum(cot * picked, axis=1, keepdims=True)
        mixed_ref[:, cols] = mixed.astype(BF16)
        rows = jnp.concatenate([ref[1, :, cols] for ref in results], axis=0)
        token_ref[:, cols] = dot_nn(turned_sum, rows).astype(BF16)
    dots_ref[...] = jnp.concatenate(
        [jnp.sum(jnp.where(eye, dot, 0.0), axis=0, keepdims=True) for dot in dots], axis=0
    )


def after(value, *others):
    return lax.optimization_barrier((value, others))[0]


def rows_of_core(core, count, cols, own, other):
    rows = jnp.concatenate([own, other], axis=0).reshape(-1, count, 2, cols)
    return lax.dynamic_index_in_dim(rows, core, 2, keepdims=False)


def down_shares(order, cols, act, act_other, c_rows, c_other):
    total, ff = act.shape
    width = c_rows.shape[1]
    count = order.shape[0]
    block = pl.BlockSpec((total, cols), lambda n, order_ref: (0, order_ref[n]))
    return pl.pallas_call(
        down_share,
        out_shape=[jax.ShapeDtypeStruct((ff, cols), BF16)] * count,
        grid_spec=pltpu.PrefetchScalarGridSpec(
            num_scalar_prefetch=1,
            grid=(count,),
            in_specs=[whole((total, ff))] * 2 + [block] * 2,
            out_specs=[whole((ff, cols))] * count,
            scratch_shapes=[pltpu.VMEM((ff, 2 * total), BF16)],
        ),
        compiler_params=params(),
        cost_estimate=cost(2 * total * width * ff, 5e6),
        name="down_shares",
    )(order, act, act_other, c_rows, c_other)


def gate_up_shares(order, cols, x_rows, x_other, grads, grads_other):
    total, width = x_rows.shape
    ff = grads.shape[2]
    count = order.shape[0]
    tile = tile_of(ff, 256)
    columns = [
        pl.BlockSpec((total, cols), lambda j, order_ref, n=n: (0, order_ref[n])) for n in range(count)
    ]
    return pl.pallas_call(
        functools.partial(gate_up_share, count),
        out_shape=[jax.ShapeDtypeStruct((cols, ff), BF16)] * (2 * count),
        grid_spec=pltpu.PrefetchScalarGridSpec(
            num_scalar_prefetch=1,
            grid=(ff // tile,),
            in_specs=columns * 2 + [pl.BlockSpec((2, total, tile), lambda j, _: (0, 0, j))] * 2,
            out_specs=[pl.BlockSpec((cols, tile), lambda j, _: (0, j))] * (2 * count),
            scratch_shapes=[pltpu.VMEM((count * cols, 2 * total), BF16)],
        ),
        compiler_params=params(),
        cost_estimate=cost(4 * total * width * ff, 9e6),
        name="gate_up_shares",
    )(order, *[x_rows] * count, *[x_other] * count, grads, grads_other)


def add(part, own):
    return (part.astype(F32) + own.astype(F32)).astype(BF16)


class LineSum:
    def __init__(self, share, chips, chip):
        self.share, self.chips, self.chip = share, chips, chip
        self.got = None
        self.steps = 0

    def share_at(self, index):
        index = jnp.clip(index, 0, self.chips - 1)
        return lax.dynamic_index_in_dim(self.share, index, 0, keepdims=False)

    def pairs(self, s):
        last = self.chips - 1
        up = [(i, i + 1) for i in range(s)]
        down = [(last - a, last - b) for a, b in up]
        return [[(2 * a + c, 2 * b + c) for a, b in way for c in (0, 1)] for way in (up, down)]

    def message(self, index, side):
        own = self.share_at(index)
        return own if self.got is None else add(self.got[side], own)

    def step(self):
        self.steps += 1
        s, chip, chips = self.steps, self.chip, self.chips
        up, down = self.pairs(s)
        if 2 * s < chips - 1:
            index = jnp.where(chip < s, chips - s + chip, chip - chips + s)
            sent = lax.ppermute(self.message(index, 0), "dp", up + down)
            self.got = (sent, sent)
        else:
            self.got = (
                lax.ppermute(self.message(chips - s + chip, 0), "dp", up),
                lax.ppermute(self.message(chip - chips + s, 1), "dp", down),
            )

    def total(self):
        own = self.share_at(self.chip).astype(F32)
        return (own + self.got[0].astype(F32) + self.got[1].astype(F32)).astype(BF16)


def relocated(total, turn, partner, me, groups):
    if turn is not None:
        return lax.ppermute(total, "expert", [(i, i ^ turn) for i in range(groups)]).astype(F32)[None]
    is_mate = (partner == me)[:, None, None]
    parts = jnp.where(is_mate, total[None], jnp.zeros_like(total)[None])
    parts = lax.all_to_all(parts, "expert", split_axis=0, concat_axis=0, tiled=True)
    mate = lax.dynamic_index_in_dim(partner, me, 0, keepdims=False)
    return lax.dynamic_index_in_dim(parts, mate, 0, keepdims=True).astype(F32)


def shards(tokens, cotangent, expert_ids, gate_weights, partner, w_gate, w_up, w_down):
    args = (tokens, cotangent, expert_ids.T, gate_weights.T, partner, w_gate, w_up, w_down)
    if lax.axis_size("expert") == 4:
        turns = [functools.partial(layer, turn) for turn in (1, 2, 3)]
        return lax.switch(partner[0] - 1, turns, *args)
    return layer(None, *args)


def layer(turn, tokens, cotangent, ids, gates, partner, w_gate, w_up, w_down):
    groups = lax.axis_size("expert")
    replicas = lax.axis_size("dp")
    me = lax.axis_index("expert")
    replica = lax.axis_index("dp")
    chips, chip, core = replicas // 2, replica // 2, replica % 2
    count, width = tokens.shape
    top = ids.shape[0]
    ff = w_gate.shape[2]
    cap = min(count, 5 * count * top // (4 * groups))
    total = groups * cap
    cols = width // replicas
    me_arr = me.astype(jnp.int32).reshape(1)
    smem = pl.BlockSpec(memory_space=pltpu.SMEM)
    vmem = pl.BlockSpec(memory_space=pltpu.VMEM)
    block_shape = jax.ShapeDtypeStruct((cap, width), BF16)

    def exchange(blocks):
        return [blocks[0]] + [
            lax.ppermute(blocks[b], "expert", [(i, i ^ b) for i in range(groups)])
            for b in range(1, groups)
        ]

    def swap(part):
        return lax.ppermute(part, "dp", [(i, i ^ 1) for i in range(replicas)])

    def joined(blocks, name):
        return pl.pallas_call(
            join,
            out_shape=jax.ShapeDtypeStruct((total, blocks[0].shape[1]), BF16),
            in_specs=[vmem] * groups,
            out_specs=vmem,
            compiler_params=params(),
            cost_estimate=cost(0, 4 * total * blocks[0].shape[1]),
            name=name,
        )(*blocks)

    x_blocks = pl.pallas_call(
        functools.partial(place_tokens, cap, groups),
        out_shape=[block_shape] * groups,
        in_specs=[smem, vmem, vmem],
        out_specs=[vmem] * groups,
        compiler_params=params(),
        name="place_tokens",
    )(me_arr, ids, tokens)
    c_blocks = pl.pallas_call(
        functools.partial(place_grads, cap, groups),
        out_shape=[block_shape] * groups,
        in_specs=[smem, vmem, vmem, vmem],
        out_specs=[vmem] * groups,
        compiler_params=params(),
        name="place_grads",
    )(me_arr, ids, gates, cotangent)
    x_blocks = exchange(x_blocks)
    c_blocks = exchange(c_blocks)

    tile = tile_of(ff, 256)
    x_rows, pre, act = pl.pallas_call(
        functools.partial(forward, cap, groups),
        out_shape=[
            jax.ShapeDtypeStruct((total, width), BF16),
            jax.ShapeDtypeStruct((2, total, ff), F32),
            jax.ShapeDtypeStruct((total, ff), BF16),
        ],
        grid=(ff // tile,),
        in_specs=[whole((cap, width))] * groups
        + [pl.BlockSpec((1, width, tile), lambda j: (0, 0, j))] * 2,
        out_specs=[
            whole((total, width)),
            pl.BlockSpec((2, total, tile), lambda j: (0, 0, j)),
            pl.BlockSpec((total, tile), lambda j: (0, j)),
        ],
        compiler_params=params(),
        cost_estimate=cost(4 * total * width * ff, 10e6),
        name="forward",
    )(*x_blocks, w_gate, w_up)
    act_other = swap(act)

    wide = tile_of(width, 1024)

    def run_backward(c_rows):
        return pl.pallas_call(
            backward,
            out_shape=jax.ShapeDtypeStruct((2, total, ff), BF16),
            grid=(ff // tile,),
            in_specs=[
                whole((total, width)),
                pl.BlockSpec((1, tile, width), lambda j: (0, j, 0)),
                pl.BlockSpec((2, total, tile), lambda j: (0, 0, j)),
            ],
            out_specs=pl.BlockSpec((2, total, tile), lambda j: (0, 0, j)),
            compiler_params=params(),
            cost_estimate=cost(2 * total * width * ff, 10e6),
            name="backward",
        )(c_rows, w_down, pre)

    def run_result_rows(act, grads):
        return pl.pallas_call(
            functools.partial(result_rows, cap),
            out_shape=[jax.ShapeDtypeStruct((2, cap, width), BF16)] * groups,
            grid=(width // wide,),
            in_specs=[
                whole((total, ff)),
                whole((2, total, ff)),
                pl.BlockSpec((1, ff, wide), lambda j: (0, 0, j)),
                pl.BlockSpec((1, wide, ff), lambda j: (0, j, 0)),
                pl.BlockSpec((1, wide, ff), lambda j: (0, j, 0)),
            ],
            out_specs=[pl.BlockSpec((2, cap, wide), lambda j: (0, 0, j))] * groups,
            compiler_params=params(),
            cost_estimate=cost(6 * total * width * ff, 13e6),
            name="result_rows",
        )(act, grads, w_down, w_gate, w_up)

    def run_combine(results):
        return pl.pallas_call(
            functools.partial(combine, cap, groups),
            out_shape=[
                jax.ShapeDtypeStruct((count, width), BF16),
                jax.ShapeDtypeStruct((count, width), BF16),
                jax.ShapeDtypeStruct((top, count), F32),
            ],
            in_specs=[smem] + [vmem] * (3 + groups),
            out_specs=[vmem] * 3,
            compiler_params=params(),
            cost_estimate=cost(6 * total * width * count, 6e6),
            name="combine",
        )(me_arr, ids, gates, cotangent, *results)

    if turn is not None and chips == 4 and cols % 128 == 0:
        low = chip < 2
        end = ((chip == 0) | (chip == 3)).astype(jnp.int32).reshape(1)
        order = (2 * jnp.where(low, 3 - jnp.arange(4), jnp.arange(4)) + core).astype(jnp.int32)

        def swap_ends(part):
            return lax.ppermute(part, "dp", [(i, i ^ 2) for i in range(replicas)])

        def swap_middle(part):
            pairs = [(2, 4), (4, 2), (3, 5), (5, 3), (0, 1), (1, 0), (6, 7), (7, 6)]
            return lax.ppermute(part, "dp", pairs)

        def to_mate(part):
            return lax.ppermute(part, "expert", [(i, i ^ turn) for i in range(groups)])

        c_rows = joined(after(c_blocks, act), "join_grads")
        c_other = swap(c_rows)
        grads = run_backward(after(c_rows, act_other))
        x_other = swap(after(x_rows, grads))
        grads_other = swap(grads)
        d_a, d_b, d_c, d_d = down_shares(order, cols, act, act_other, c_rows, after(c_other, grads))
        d_1 = swap_ends(d_a)
        d_2 = swap_ends(after(d_b, d_a))
        g_a, g_b, g_c, g_d, u_a, u_b, u_c, u_d = gate_up_shares(
            order, cols, after(x_rows, d_a), x_other, grads, grads_other
        )
        rows = run_result_rows(act, after(grads, g_a))

        m = added("down_mid1", BF16, *after((d_1, d_a), *rows))
        d_m1, g_1 = swap_middle(m), swap_ends(after(g_a, m))
        m = added("down_mid2", BF16, *after((d_2, d_b), m))
        d_m2, u_1 = swap_middle(m), swap_ends(after(u_a, m))
        results = [rows[0]]
        for n, part in enumerate(rows[1:], 1):
            part = after(part, m) if n < groups - 1 else after(part, results[-1], m)
            results.append(lax.ppermute(part, "expert", [(i, i ^ n) for i in range(groups)]))

        m = added("gate_mid1", BF16, *after((g_1, g_a), m))
        g_m1 = swap_middle(m)
        (e,) = last_share("down_last", 1, end, *after((d_c, d_m1, d_d), m))
        d_3 = swap_ends(e)
        m = added("up_mid1", BF16, *after((u_1, u_a), e, d_m2))
        u_m1, g_2 = swap_middle(m), swap_ends(after(g_b, m))
        t = final_sum("down_sum", 0, end, *after((d_3, d_d, d_c, d_m2), m, results[1]))
        d_t = to_mate(t)
        (e,) = last_share("gate_last", 1, end, *after((g_c, g_m1, g_d), t))
        g_3 = swap_ends(e)
        m = added("gate_mid2", BF16, *after((g_2, g_b), e, results[2]))
        g_m2 = swap_middle(m)
        half = u_b.shape[0] // 2
        u_b0, u_b1 = after((u_b[:half], u_b[half:]), m)
        u_20, u_21 = swap_ends(u_b0), swap_ends(u_b1)
        e0, e1 = last_share("up_last", 2, end, *after((u_c, u_m1, u_d), m))
        t = final_sum("gate_sum", 0, end, *after((g_3, g_d, g_c, g_m2), e0, d_t))
        g_t, u_30 = to_mate(t), swap_ends(after(e0, g_3))
        m0 = added("up_mid20", BF16, *after((u_20, u_b0), t))
        u_m20 = swap_middle(m0)
        m1 = added("up_mid21", BF16, *after((u_21, u_b1), m0))
        u_m21, u_31 = swap_middle(m1), swap_ends(after(e1, m0))

        mixed_out, token_grad, gate_grad = run_combine(after(results, m1))
        slot_down = slot_of("slot_down", *after((d_t,), mixed_out))
        t0 = final_sum("up_sum0", 0, end, *after((u_30, u_d, u_c, u_m20), slot_down, g_t))
        u_t0 = to_mate(t0)
        t1 = final_sum("up_sum1", 1, end, *after((u_31, u_d, u_c, u_m21), t0))
        u_t1 = to_mate(t1)
        slot_gate = slot_of("slot_gate", *after((g_t,), t1))
        slot_up = slot_of("slot_up", *after((u_t0, u_t1), slot_gate))
    else:
        c_rows = joined(c_blocks, "join_grads")
        grads = run_backward(c_rows)
        results = exchange(run_result_rows(act, grads))
        acts = jnp.concatenate([act, act_other], axis=0)
        both_grads = jnp.concatenate([grads, swap(grads)], axis=1)
        c_both = rows_of_core(core, chips, cols, c_rows, swap(c_rows))
        x_both = rows_of_core(core, chips, cols, x_rows, swap(x_rows))

        def dot(spec, left, right):
            return jnp.einsum(spec, left, right, preferred_element_type=F32).astype(BF16)

        lines = [
            LineSum(share, chips, chip)
            for share in (
                dot("rf,rzc->zfc", acts, c_both),
                dot("rzc,rf->zcf", x_both, both_grads[0]),
                dot("rzc,rf->zcf", x_both, both_grads[1]),
            )
        ]
        for _ in range(1, chips):
            for line in lines:
                line.step()
        slot_down, slot_gate, slot_up = [
            relocated(line.total(), turn, partner, me, groups) for line in lines
        ]
        mixed_out, token_grad, gate_grad = run_combine(results)

    return mixed_out, token_grad, gate_grad.T, slot_gate, slot_up, slot_down


def solution(mesh):
    rows = P(("dp", "expert"), None)
    in_specs = (
        rows,
        rows,
        rows,
        rows,
        P(),
        P("expert", None, None),
        P("expert", None, None),
        P("expert", None, None),
    )
    out_specs = (
        rows,
        rows,
        rows,
        P("expert", "dp", None),
        P("expert", "dp", None),
        P("expert", None, "dp"),
    )
    return jax.shard_map(shards, mesh=mesh, in_specs=in_specs, out_specs=out_specs, check_vma=False)
```
